128 devices in a mesh: ctx: 8 (over y, core), dec: 16 (over z, x).
Axes of the slice: x: 4, y: 4, z: 4, core: 2. Of those that a mesh axis runs over, the one named last changes fastest.
Arguments:
- queries: bfloat16 [16, 1024, 16384], P('dec', 'ctx'), may hold values from -36 to 36
- keys: bfloat16 [16, 1024, 1024], P('dec', 'ctx'), may hold values from -3 to 3
- values: bfloat16 [16, 1024, 1024], P('dec', 'ctx'), may hold values from -4 to 4
- lengths: int32 [16, 4], P('dec'), may hold values from 1 to 512, 1024 in all within a row
- owners: int32 [16, 128, 1], P('dec', 'ctx'), may hold values from 0 to 15; in each aligned block of 16 rows (0 to 15, 16 to 31, ..., all dimensions but the last counted through in order) at most 2 rows name the same one
Outputs:
- attended: bfloat16 [16, 1024, 16384], P('dec', 'ctx')
- cache_keys: bfloat16 [128, 8, 32, 1024], P(None, 'ctx', 'dec')
- cache_values: bfloat16 [128, 8, 32, 1024], P(None, 'ctx', 'dec')
- cache_key_scales: bfloat16 [128, 8, 32, 8], P(None, 'ctx', 'dec')
- cache_value_scales: bfloat16 [128, 8, 32, 8], P(None, 'ctx', 'dec')
The draws below stay inside these ranges and needn't reach their ends.
Inputs may be any that keep to these rules, and one draw needn't show every extreme that they name: `owners`: at most 2 of the 16 pages of one device go to one decode owner.
All inputs are finite; a program needn't handle non-finite values. Where the reference program divides by a largest or mean magnitude, that divisor is 1e-20 or more.
Results may differ from the reference program's by a relative error of at most 0.013.
Values may be sent and summed in bfloat16 or wider, within the bound.
No kernel may reach another device: no remote copies, remote signals or barrier semaphores. Data moves between devices by JAX's collectives and lax.ppermute only.
A program may use at most 128 MiB of HBM per device.

```python
import math
import jax
import jax.numpy as jnp
import numpy as np
from jax import lax

QH = 128
KVH = 8
HD = 128
PAGE = 8
CAP = 2
REQS = 4
SEQ = 1024
GROUPS = 16
SOURCES = 128
PAGES_DEV = 16
PAGES = 128


def draw_keys(key, part):
    key = jax.random.fold_in(key, 1)
    normal_rows = jax.random.normal(key, (GROUPS, SEQ, KVH * HD), jnp.float32)
    return jnp.clip(normal_rows, -3.0, 3.0).astype(jnp.bfloat16)


def draw_queries(key, part):
    key = jax.random.fold_in(key, 2)
    normal_rows = jax.random.normal(key, (GROUPS, SEQ, QH * HD), jnp.float32)
    return jnp.clip(normal_rows, -3.0, 3.0).astype(jnp.bfloat16)


def shard_levels(stream_key, extent, pieces, smallest, high):
    loudness, own = 1.0, jax.random.fold_in(stream_key, 6)
    for axis_at, blocks in pieces:
        heights = jnp.exp(jax.random.uniform(jax.random.fold_in(own, axis_at), (blocks,), jnp.float32, smallest / len(pieces), high / len(pieces)))
        loudness = loudness * jnp.repeat(heights, extent[axis_at] // blocks).reshape([-1 if axis == axis_at else 1 for axis in range(len(extent))])
    return loudness


def profile(amount, total, limit, lean):
    portions = [(1 << 20) // math.isqrt(standing ** lean) + 1 for standing in range(2, amount + 1)]
    surplus, counts = total - limit - (amount - 1), [1] * (amount - 1)
    while surplus > 0:
        movable = [i for i in range(amount - 1) if counts[i] < limit]
        whole, left = sum([portions[i] for i in movable]), surplus
        for i in movable:
            more = min(limit - counts[i], max(1, left * portions[i] // whole), surplus)
            counts[i] = counts[i] + more
            surplus = surplus - more
    return np.array([limit] + counts)


def ragged(rng, number_of, total, limit, slope):
    if number_of == 2:
        one = jax.random.randint(rng, (), max(1, total - limit), min(limit, total - 1) + 1)
        return jnp.stack([one, total - one])
    sizes = jnp.asarray(profile(number_of, total, limit, slope), jnp.int32)
    pairs = (number_of - 1) // 2
    donor, taker = sizes[1:1 + 2 * pairs:2], sizes[2:2 + 2 * pairs:2]
    room = jnp.minimum(donor - 1, limit - taker)
    moved = jax.random.randint(jax.random.fold_in(rng, 1), (pairs,), 0, 1 << 20) % (room + 1)
    sizes = sizes.at[1:1 + 2 * pairs:2].set(donor - moved).at[2:2 + 2 * pairs:2].set(taker + moved)
    return sizes[jax.random.permutation(jax.random.fold_in(rng, 2), number_of)]


def routed_block(key, own, number, rows, number_of, top, bound, slope):
    ranking = jax.random.permutation(key, number_of)
    packed, ordinary = load_shares(number_of, rows * top, bound, slope, True), load_shares(number_of, rows * top, bound, slope, False)
    places = jnp.arange(number_of)

    def named(sizes, offset_by):
        used = int((sizes > 0).sum())
        fixed = max(1, used // 4)
        passed = fixed + (places - fixed + offset_by * (used - fixed)) % max(1, number_of - fixed)
        return jnp.zeros((number_of,), jnp.int32).at[ranking[jnp.where(places < fixed, places, passed)]].set(jnp.asarray(sizes, jnp.int32))

    sizes = jnp.where(number % 4 == 0, named(packed, number // 4), named(ordinary, number - number // 4 - 1))
    mixed = jax.random.permutation(jax.random.fold_in(own, 3), number_of)
    donor, receiver = mixed[0:number_of // 2 * 2:2], mixed[1:number_of // 2 * 2:2]
    margin = jnp.minimum(sizes[donor] - 1, bound - sizes[receiver]) // 2
    margin = jnp.where((donor == ranking[0]) | (receiver == ranking[0]) | (sizes[receiver] == 0), 0, jnp.maximum(margin, 0))
    passed = jax.random.randint(jax.random.fold_in(own, 4), (number_of // 2,), 0, 1 << 20) % (margin + 1)
    sizes = sizes.at[donor].add(-passed).at[receiver].add(passed)
    items = jnp.searchsorted(jnp.cumsum(sizes), jnp.arange(rows * top), side="right").astype(jnp.int32)
    table = items.reshape(top, rows).T
    table = table[jax.random.permutation(jax.random.fold_in(own, 1), rows)]
    offset_by = jax.random.randint(jax.random.fold_in(own, 2), (rows, 1), 0, top)
    return jnp.take_along_axis(table, (jnp.arange(top)[None, :] + offset_by) % top, axis=1)


def load_shares(count, total, reach, slope, full):
    portions = [(1 << 20) // math.isqrt(grade ** slope) + 1 for grade in range(1, count + 1)]
    largest = reach if full else min(reach, max(-(-total // count), total * portions[0] // sum(portions)))
    least = 1 if total - largest >= count - 1 else 0
    holding, surplus = [largest] + [least] * (count - 1), total - largest - least * (count - 1)
    while surplus > 0:
        movable = [i for i in range(1, count) if holding[i] < largest] or [i for i in range(1, count) if holding[i] < reach]
        pool, budget = sum([portions[i] for i in movable]), surplus
        for i in movable:
            addition = min(reach - holding[i], max(1, budget * portions[i] // pool), surplus)
            holding[i] = holding[i] + addition
            surplus = surplus - addition
    return np.array(holding)


def bell_draw(own_key, shape, spread, bound, split=(), kind=jnp.bfloat16):
    array = jax.random.normal(own_key, shape, jnp.float32) * spread
    if len(split) > 0:
        array = shard_levels(own_key, shape, split, -0.22, 0.18) * array
    return jnp.clip(array, min=-bound, max=bound).astype(kind)


def setup_inputs(seed: int = 0) -> dict:
    arg_keys = jax.random.split(jax.random.key(seed), 6)
    queries = draw_queries(jax.random.fold_in(arg_keys[5], 71), 0)
    keys = draw_keys(jax.random.fold_in(arg_keys[5], 71), 0)
    values = bell_draw(arg_keys[2], (GROUPS, SEQ, KVH * HD), 1.0, 4.0, ((0, 16), (1, 8)))
    lengths = jax.vmap(lambda own: ragged(own, REQS, SEQ, SEQ // 2, 2))(jax.random.split(arg_keys[3], GROUPS)).reshape((GROUPS, REQS)).astype(jnp.int32)
    owners_keys = jax.random.split(jax.random.fold_in(arg_keys[4], 1), GROUPS * PAGES // PAGES_DEV)
    owners_turns = jax.random.permutation(jax.random.fold_in(arg_keys[4], 3), GROUPS * PAGES // PAGES_DEV)
    owners = jax.vmap(lambda own, number: routed_block(jax.random.fold_in(arg_keys[4], 2), own, number, PAGES_DEV, GROUPS, 1, CAP, 2))(owners_keys, owners_turns).reshape((GROUPS, PAGES, 1))
    return {"queries": queries, "keys": keys, "values": values, "lengths": lengths, "owners": owners}


def hadamard_signs():
    row_index = lax.broadcasted_iota(jnp.int32, (HD, HD), 0)
    col_index = lax.broadcasted_iota(jnp.int32, (HD, HD), 1)
    common = row_index & col_index
    parity = jnp.zeros((HD, HD), jnp.int32)
    for bit_number in range(HD.bit_length()):
        parity = parity + (common >> bit_number & 1)
    return (1 - 2 * (parity % 2)).astype(jnp.bfloat16)

def rotate_codes(rows_block):
    rotated = jnp.dot(rows_block, hadamard_signs(), preferred_element_type=jnp.float32) * (1.0 / math.sqrt(HD))
    block_scale = (lax.optimization_barrier(jnp.max(jnp.abs(rotated), axis=-1)) + 1e-06).astype(jnp.bfloat16)
    codes = (rotated / block_scale.astype(jnp.float32)[:, None]).astype(jnp.bfloat16)
    return (codes, block_scale)

def request_of(positions, request_ends):
    return lax.optimization_barrier(jnp.sum((positions[:, None] >= request_ends[None, :]).astype(jnp.int32), axis=1))

def group_attention(query_rows, key_rows, value_rows, lengths_row):
    group_size = QH // KVH
    positions = jnp.arange(SEQ, dtype=jnp.int32)
    request_ends = jnp.cumsum(lengths_row).astype(jnp.int32)
    request = request_of(positions, request_ends)
    allowed = (request[:, None] == request[None, :]) & (positions[None, :] <= positions[:, None])
    query_heads = query_rows.reshape(SEQ, KVH, group_size, HD).transpose(1, 2, 0, 3).reshape(KVH, group_size * SEQ, HD)
    key_heads = key_rows.reshape(SEQ, KVH, HD).transpose(1, 0, 2)
    value_heads = value_rows.reshape(SEQ, KVH, HD).transpose(1, 0, 2)
    inv_root = 1.0 / math.sqrt(HD)

    def one_head(head_items):
        query_block, key_block, value_block = head_items
        scores = jnp.dot(query_block, key_block.T, preferred_element_type=jnp.float32) * inv_root
        scores = scores.reshape(group_size, SEQ, SEQ)
        masked = jnp.where(allowed[None], scores, -1e+30)
        row_top = lax.optimization_barrier(jnp.max(masked, axis=-1, keepdims=True))
        weights = jnp.where(allowed[None], jnp.exp(scores - row_top), 0.0)
        row_total = lax.optimization_barrier(jnp.sum(weights, axis=-1)).reshape(group_size * SEQ)
        mixed = jnp.dot(weights.astype(jnp.bfloat16).reshape(group_size * SEQ, SEQ), value_block, preferred_element_type=jnp.float32)
        return (mixed / row_total[:, None]).astype(jnp.bfloat16)
    heads_out = lax.map(one_head, (query_heads, key_heads, value_heads))
    return heads_out.reshape(KVH, group_size, SEQ, HD).transpose(2, 0, 1, 3).reshape(SEQ, QH * HD)

def page_cache(source_rows, source_index, slot_index, last_width):
    cache = jnp.zeros((SOURCES, KVH, GROUPS * CAP, last_width), source_rows.dtype)
    return cache.at[source_index, :, slot_index].set(source_rows)

def reference(queries, keys, values, lengths, owners):
    attended = lax.map(lambda group_items: group_attention(*group_items), (queries, keys, values, lengths))
    key_codes, key_scale = rotate_codes(keys.reshape(-1, HD))
    value_codes, value_scale = rotate_codes(values.reshape(-1, HD))

    def to_pages(codes):
        return codes.reshape(GROUPS, PAGES, PAGE, KVH, HD).transpose(0, 1, 3, 2, 4).reshape(GROUPS, PAGES, KVH, PAGE * HD)

    def scale_pages(block_scale):
        return block_scale.reshape(GROUPS, PAGES, PAGE, KVH).transpose(0, 1, 3, 2)
    owner = owners[:, :, 0]
    page_index = jnp.arange(PAGES, dtype=jnp.int32)
    device_of = page_index // PAGES_DEV
    earlier = (owner[:, :, None] == owner[:, None, :]) & (device_of[None, :, None] == device_of[None, None, :]) & (page_index[None, None, :] < page_index[None, :, None])
    rank = lax.optimization_barrier(jnp.sum(earlier.astype(jnp.int32), axis=2)).astype(jnp.int32)
    source_index = (device_of[None, :] * GROUPS + jnp.arange(GROUPS, dtype=jnp.int32)[:, None]).astype(jnp.int32)
    slot_index = (owner * CAP + rank).astype(jnp.int32)
    cache_keys = page_cache(to_pages(key_codes), source_index, slot_index, PAGE * HD)
    cache_values = page_cache(to_pages(value_codes), source_index, slot_index, PAGE * HD)
    cache_key_scales = page_cache(scale_pages(key_scale), source_index, slot_index, PAGE)
    cache_value_scales = page_cache(scale_pages(value_scale), source_index, slot_index, PAGE)
    return (attended, cache_keys, cache_values, cache_key_scales, cache_value_scales)
```

```python
import functools
import math

import jax
import jax.numpy as jnp
from jax import lax
from jax.experimental import pallas as pl
from jax.experimental.pallas import tpu as pltpu
from jax.sharding import PartitionSpec as P

HD = 128
KVH = 8
GROUP = 16
PAGE = 8
CAP = 2
REQS = 4
TOK = 128
PAGES_DEV = 16
OWNERS = 16
BLOCKS = 5
WINDOW = BLOCKS * TOK
ROW = 2 * PAGE * HD + HD
STACK = 2
PARTS = ((0, 5), (5, 3))
EXP_SCALE = math.log2(math.e) / math.sqrt(HD)
INV_ROOT = 1.0 / math.sqrt(HD)
NT = (((1,), (1,)), ((), ()))
NN = (((1,), (0,)), ((), ()))
ANY = pl.BlockSpec(memory_space=pl.ANY)
SMEM = pl.BlockSpec(memory_space=pltpu.SMEM)
VMEM = pl.BlockSpec(memory_space=pltpu.VMEM)


def iota(shape, axis):
    return lax.broadcasted_iota(jnp.int32, shape, axis)


def pack_kernel(owners, keys, values, out):
    row, col = iota((HD, HD), 0), iota((HD, HD), 1)
    common = row & col
    parity = jnp.zeros((HD, HD), jnp.int32)
    for bit in range(7):
        parity = parity + ((common >> bit) & 1)
    signs = (1 - 2 * (parity & 1)).astype(jnp.float32).astype(jnp.bfloat16)
    position = iota((1, TOK), 1)
    page, within = position // PAGE, position % PAGE
    slot = jnp.zeros((1, TOK), jnp.int32)
    for p in range(PAGES_DEV):
        rank = jnp.int32(0)
        for q in range(p):
            rank = rank + (owners[q] == owners[p]).astype(jnp.int32)
        slot = jnp.where(page == p, owners[p] * CAP + rank, slot)
    slots = OWNERS * CAP
    place = iota((PAGE * slots, TOK), 0)
    select = jnp.where((place % slots == slot) & (place // slots == within), 1.0, 0.0).astype(jnp.bfloat16)
    any_row = jnp.where(iota((slots, TOK), 0) == slot, 1.0, 0.0).astype(jnp.bfloat16)
    lane, in_page = iota((TOK, HD), 1), iota((TOK, HD), 0) % PAGE
    for h in range(KVH):
        scales = jnp.zeros((TOK, HD), jnp.float32)
        for which, rows in enumerate((keys, values)):
            rotated = (
                lax.dot_general(rows[0, :, h * HD : (h + 1) * HD], signs, NN, preferred_element_type=jnp.float32)
                * INV_ROOT
            )
            scale = (jnp.max(jnp.abs(rotated), axis=-1, keepdims=True) + 1e-06).astype(jnp.bfloat16)
            scale = scale.astype(jnp.float32)
            codes = (rotated / scale).astype(jnp.bfloat16)
            placed = lax.dot_general(select, codes, NN, preferred_element_type=jnp.float32).astype(jnp.bfloat16)
            for i in range(PAGE):
                at = (which * PAGE + i) * HD
                out[h, :, at : at + HD] = placed[i * slots : (i + 1) * slots]
            scales = jnp.where(lane == which * PAGE + in_page, scale, scales)
        out[h, :, 2 * PAGE * HD :] = lax.dot_general(
            any_row, scales.astype(jnp.bfloat16), NN, preferred_element_type=jnp.float32
        ).astype(jnp.bfloat16)


def pack(owners, keys, values):
    return pl.pallas_call(
        pack_kernel,
        in_specs=[SMEM, VMEM, VMEM],
        out_specs=VMEM,
        out_shape=jax.ShapeDtypeStruct((KVH, OWNERS * CAP, ROW), jnp.bfloat16),
        compiler_params=pltpu.CompilerParams(vmem_limit_bytes=24 * 2**20),
        cost_estimate=pl.CostEstimate(flops=2 * 10**8, bytes_accessed=2 * 10**6, transcendentals=0),
        name="pack",
    )(owners, keys, values)


def attend_kernel(first, heads, where, queries, own, near, far, swapped, *rest):
    out, q_buf, o_buf, k_buf, v_buf, bias, q_sem, kv_sem, o_sem = rest[-9:]
    head_width = GROUP * HD

    def query_copy(h):
        at = pl.ds(pl.multiple_of(h * head_width, head_width), head_width)
        from_at = pl.ds(pl.multiple_of((first + h) * head_width, head_width), head_width)
        return pltpu.make_async_copy(queries.at[0, :, from_at], q_buf.at[:, at], q_sem.at[h])

    def out_copy(h):
        at = pl.ds(pl.multiple_of(h * head_width, head_width), head_width)
        to_at = pl.ds(pl.multiple_of((first + h) * head_width, head_width), head_width)
        return pltpu.make_async_copy(o_buf.at[:, at], out.at[0, :, to_at], o_sem.at[h])

    blocks = (far, swapped.at[0], near, swapped.at[1], own)
    kv_copies = []
    for b, block in enumerate(blocks):
        for which, buf in enumerate((k_buf, v_buf)):
            kv_copies.append(
                pltpu.make_async_copy(block.at[which], buf.at[pl.ds(b * TOK, TOK)], kv_sem.at[2 * b + which])
            )
    for copy in kv_copies:
        copy.start()
    for h in range(heads):
        query_copy(h).start()

    ctx = where[0]
    core = lax.rem(ctx, 2)
    query_pos = ctx * TOK + iota((TOK, TOK), 0)
    start = jnp.zeros((TOK, TOK), jnp.int32)
    end = jnp.int32(0)
    for r in range(REQS):
        end = end + where[1 + r]
        start = jnp.where(query_pos >= end, end, start)
    back = (4, jnp.where(core == 0, 3, 1), 2, jnp.where(core == 0, 1, 3), 0)
    for b in range(BLOCKS):
        key_pos = (ctx - back[b]) * TOK + iota((TOK, TOK), 1)
        kept = (key_pos >= start) & (key_pos <= query_pos)
        bias[b * TOK : (b + 1) * TOK, :] = jnp.where(kept, 0.0, -1e30).astype(jnp.bfloat16).T
    eye = jnp.where(iota((TOK, TOK), 0) == iota((TOK, TOK), 1), 1.0, 0.0).astype(jnp.bfloat16)
    eyes = jnp.concatenate([eye] * STACK, 0)
    ones = jnp.ones((WINDOW, HD), jnp.bfloat16)
    for copy in kv_copies:
        copy.wait()

    def one_head(h, carry):
        query_copy(h).wait()
        lanes = pl.ds(pl.multiple_of(h * HD, HD), HD)
        key_side = jnp.concatenate([k_buf[:, lanes], bias[...]], 1)
        value_side = jnp.concatenate([v_buf[:, lanes], ones], 1)

        def head_lanes(g):
            return pl.ds(pl.multiple_of(h * head_width + g * HD, HD), HD)

        def score(g0):
            rows = jnp.concatenate([q_buf[:, head_lanes(g0 + g)] for g in range(STACK)], 0)
            return lax.dot_general(
                jnp.concatenate([rows, eyes], 1), key_side, NT, preferred_element_type=jnp.float32
            )

        def finish(g0, scores):
            top = jnp.max(scores, axis=-1, keepdims=True)
            weights = jnp.exp2((scores - top) * EXP_SCALE).astype(jnp.bfloat16)
            mixed = lax.dot_general(weights, value_side, NN, preferred_element_type=jnp.float32)
            result = (mixed[:, :HD] / mixed[:, HD:]).astype(jnp.bfloat16)
            for g in range(STACK):
                o_buf[:, head_lanes(g0 + g)] = result[g * TOK : (g + 1) * TOK]

        scores = score(0)
        for g0 in range(0, GROUP, STACK):
            following = score(g0 + STACK) if g0 + STACK < GROUP else None
            finish(g0, scores)
            scores = following
        out_copy(h).start()
        return carry

    lax.fori_loop(0, heads, one_head, 0)
    for h in range(heads):
        out_copy(h).wait()


def attend(first, heads, where, queries, own, near, far, swapped, partial):
    more = () if partial is None else (partial,)
    scores = GROUP * TOK * WINDOW * heads
    return pl.pallas_call(
        functools.partial(attend_kernel, first, heads),
        in_specs=[SMEM] + [ANY] * (5 + len(more)),
        out_specs=ANY,
        out_shape=jax.ShapeDtypeStruct(queries.shape, jnp.bfloat16),
        scratch_shapes=[
            pltpu.VMEM((TOK, heads * GROUP * HD), jnp.bfloat16),
            pltpu.VMEM((TOK, heads * GROUP * HD), jnp.bfloat16),
            pltpu.VMEM((WINDOW, heads * HD), jnp.bfloat16),
            pltpu.VMEM((WINDOW, heads * HD), jnp.bfloat16),
            pltpu.VMEM((WINDOW, TOK), jnp.bfloat16),
            pltpu.SemaphoreType.DMA((heads,)),
            pltpu.SemaphoreType.DMA((2 * BLOCKS,)),
            pltpu.SemaphoreType.DMA((heads,)),
        ],
        input_output_aliases={6: 0} if more else {},
        compiler_params=pltpu.CompilerParams(vmem_limit_bytes=32 * 2**20),
        cost_estimate=pl.CostEstimate(
            flops=scores * HD * 6, bytes_accessed=2 * heads * GROUP * TOK * HD * 2, transcendentals=scores
        ),
        name=f"attend{first}",
    )(where, queries, own, near, far, swapped, *more)


def body(queries, keys, values, lengths, owners):
    ctx_index = lax.axis_index("ctx")
    ctx_count = lax.axis_size("ctx")
    where = jnp.concatenate([ctx_index.astype(jnp.int32).reshape(1), lengths[0]])

    def chips_on(block, chips):
        step = 2 * chips
        return lax.ppermute(block, "ctx", [(i, i + step) for i in range(ctx_count - step)])

    owns, nears, fars = [], [], []
    for first, heads in PARTS:
        lanes = slice(first * HD, (first + heads) * HD)
        own = jnp.concatenate([keys[:, :, lanes], values[:, :, lanes]], 0)
        owns.append(own)
        nears.append(chips_on(own, 1))
        fars.append(chips_on(own, 2))

    message = pack(owners.reshape(PAGES_DEV), keys, values)
    message = message.reshape(KVH * OWNERS, CAP, ROW)
    received = lax.all_to_all(message, ("ctx", "dec"), split_axis=0, concat_axis=0, tiled=True)

    attended = None
    for (first, heads), own, near, far in zip(PARTS, owns, nears, fars):
        handed = jnp.where(ctx_index % 2 == 0, own, far)
        swapped = lax.ppermute(jnp.stack([handed, near]), "ctx", [(i, i ^ 1) for i in range(ctx_count)])
        attended = attend(first, heads, where, queries, own, near, far, swapped, attended)

    half = PAGE * HD
    cache_keys = received[:, None, :, :half]
    cache_values = received[:, None, :, half : 2 * half]
    key_scales = received[:, None, :, 2 * half : 2 * half + PAGE]
    value_scales = received[:, None, :, 2 * half + PAGE : 2 * half + 2 * PAGE]
    return (attended, cache_keys, cache_values, key_scales, value_scales)


def solution(mesh):
    placed = (
        P("dec", "ctx", None),
        P("dec", "ctx", None),
        P("dec", "ctx", None),
        P("dec", None),
        P("dec", "ctx", None),
    )
    return jax.shard_map(
        body,
        mesh=mesh,
        in_specs=placed,
        out_specs=(
            P("dec", "ctx", None),
            P(None, "ctx", "dec", None),
            P(None, "ctx", "dec", None),
            P(None, "ctx", "dec", None),
            P(None, "ctx", "dec", None),
        ),
        check_vma=False,
    )
```

```python
import functools
import math

import jax
import jax.numpy as jnp
from jax import lax
from jax.experimental import pallas as pl
from jax.experimental.pallas import tpu as pltpu
from jax.sharding import PartitionSpec as P

HD = 128
KVH = 8
GROUP = 16
PAGE = 8
CAP = 2
REQS = 4
TOK = 128
PAGES_DEV = 16
OWNERS = 16
BLOCKS = 5
WINDOW = BLOCKS * TOK
ROW = 2 * PAGE * HD + HD
STACK = 8
STACK_TOP = 4
HEAD_WIDTH = GROUP * HD
SUM_LEAST = 2.0**-100
SUM_MOST = 2.0**100
PARTS = ((0, 8),)
EXP_SCALE = math.log2(math.e) / math.sqrt(HD)
INV_ROOT = 1.0 / math.sqrt(HD)
NT = (((1,), (1,)), ((), ()))
NN = (((1,), (0,)), ((), ()))
CHEAP = pl.CostEstimate(flops=1000, bytes_accessed=1000, transcendentals=0)
HBM = pl.BlockSpec(memory_space=pltpu.HBM)
SMEM = pl.BlockSpec(memory_space=pltpu.SMEM)
VMEM = pl.BlockSpec(memory_space=pltpu.VMEM)


def iota(shape, axis):
    return lax.broadcasted_iota(jnp.int32, shape, axis)


def pack_kernel(owners, keys, values, out):
    row, col = iota((HD, HD), 0), iota((HD, HD), 1)
    common = row & col
    parity = jnp.zeros((HD, HD), jnp.int32)
    for bit in range(7):
        parity = parity + ((common >> bit) & 1)
    signs = (1 - 2 * (parity & 1)).astype(jnp.float32).astype(jnp.bfloat16)
    position = iota((1, TOK), 1)
    page, within = position // PAGE, position % PAGE
    slot = jnp.zeros((1, TOK), jnp.int32)
    for p in range(PAGES_DEV):
        rank = jnp.int32(0)
        for q in range(p):
            rank = rank + (owners[q] == owners[p]).astype(jnp.int32)
        slot = jnp.where(page == p, owners[p] * CAP + rank, slot)
    slots = OWNERS * CAP
    place = iota((PAGE * slots, TOK), 0)
    select = jnp.where((place % slots == slot) & (place // slots == within), 1.0, 0.0).astype(jnp.bfloat16)
    any_row = jnp.where(iota((slots, TOK), 0) == slot, 1.0, 0.0).astype(jnp.bfloat16)
    lane, in_page = iota((TOK, HD), 1), iota((TOK, HD), 0) % PAGE
    for h in range(KVH):
        scales = jnp.zeros((TOK, HD), jnp.float32)
        for which, rows in enumerate((keys, values)):
            rotated = (
                lax.dot_general(rows[0, :, h * HD : (h + 1) * HD], signs, NN, preferred_element_type=jnp.float32)
                * INV_ROOT
            )
            scale = (jnp.max(jnp.abs(rotated), axis=-1, keepdims=True) + 1e-06).astype(jnp.bfloat16)
            scale = scale.astype(jnp.float32)
            codes = (rotated / scale).astype(jnp.bfloat16)
            placed = lax.dot_general(select, codes, NN, preferred_element_type=jnp.float32).astype(jnp.bfloat16)
            for i in range(PAGE):
                at = (which * PAGE + i) * HD
                out[h, :, at : at + HD] = placed[i * slots : (i + 1) * slots]
            scales = jnp.where(lane == which * PAGE + in_page, scale, scales)
        out[h, :, 2 * PAGE * HD :] = lax.dot_general(
            any_row, scales.astype(jnp.bfloat16), NN, preferred_element_type=jnp.float32
        ).astype(jnp.bfloat16)


def pack(owners, keys, values):
    return pl.pallas_call(
        pack_kernel,
        in_specs=[SMEM, VMEM, VMEM],
        out_specs=VMEM,
        out_shape=jax.ShapeDtypeStruct((KVH, OWNERS * CAP, ROW), jnp.bfloat16),
        compiler_params=pltpu.CompilerParams(vmem_limit_bytes=24 * 2**20),
        cost_estimate=CHEAP,
        name="pack",
    )(owners, keys, values)


def unpack_kernel(received, cache_keys, cache_values, key_scales, value_scales, sem):
    half = PAGE * HD
    copies = [
        pltpu.make_async_copy(received.at[:, :, pl.ds(0, half)], cache_keys.at[:, 0], sem.at[0]),
        pltpu.make_async_copy(received.at[:, :, pl.ds(half, half)], cache_values.at[:, 0], sem.at[1]),
    ]
    for copy in copies:
        copy.start()
    for slot in range(CAP):
        turned = received[:, slot, 2 * half :].T
        key_scales[slot] = turned[:PAGE]
        value_scales[slot] = turned[PAGE : 2 * PAGE]
    for copy in copies:
        copy.wait()


def unpack(received):
    sources = received.shape[0]
    cache = jax.ShapeDtypeStruct((sources, 1, CAP, PAGE * HD), jnp.bfloat16)
    scales = jax.ShapeDtypeStruct((CAP, PAGE, sources), jnp.bfloat16)
    cache_keys, cache_values, key_scales, value_scales = pl.pallas_call(
        unpack_kernel,
        in_specs=[VMEM],
        out_specs=[HBM, HBM, VMEM, VMEM],
        out_shape=[cache, cache, scales, scales],
        scratch_shapes=[pltpu.SemaphoreType.DMA((2,))],
        cost_estimate=CHEAP,
        name="unpack",
    )(received)
    return (
        cache_keys,
        cache_values,
        key_scales.transpose(2, 0, 1)[:, None],
        value_scales.transpose(2, 0, 1)[:, None],
    )


def attend_kernel(first, heads, where, queries, keys, values, near_keys, near_values, far_keys, far_values, swapped, *rest):
    out, q_buf, o_buf, bias, sums, q_sem, o_sem = rest[-7:]
    key_blocks = (far_keys, swapped.at[0], near_keys, swapped.at[1], keys)
    value_blocks = (far_values, swapped.at[2], near_values, swapped.at[3], values)

    def query_copy(h):
        at = pl.ds(pl.multiple_of(h * HEAD_WIDTH, HEAD_WIDTH), HEAD_WIDTH)
        from_at = pl.ds(pl.multiple_of((first + h) * HEAD_WIDTH, HEAD_WIDTH), HEAD_WIDTH)
        return pltpu.make_async_copy(queries.at[0, :, from_at], q_buf.at[:, at], q_sem.at[h])

    def out_copy(h, g0):
        width = STACK * HD
        at = pl.ds(pl.multiple_of(h * HEAD_WIDTH + g0 * HD, width), width)
        to_at = pl.ds(pl.multiple_of((first + h) * HEAD_WIDTH + g0 * HD, width), width)
        return pltpu.make_async_copy(o_buf.at[:, at], out.at[0, :, to_at], o_sem.at[h])

    for h in range(heads):
        query_copy(h).start()

    ctx = where[0]
    core = lax.rem(ctx, 2)
    query_pos = ctx * TOK + iota((TOK, TOK), 1)
    start = jnp.zeros((TOK, TOK), jnp.int32)
    end = jnp.int32(0)
    for r in range(REQS):
        end = end + where[1 + r]
        start = jnp.where(query_pos >= end, end, start)
    back = (4, jnp.where(core == 0, 3, 1), 2, jnp.where(core == 0, 1, 3), 0)
    for b in range(BLOCKS):
        key_pos = (ctx - back[b]) * TOK + iota((TOK, TOK), 0)
        kept = (key_pos >= start) & (key_pos <= query_pos)
        bias[b * TOK : (b + 1) * TOK, :] = jnp.where(kept, 0.0, -1e30)
    sums[0] = jnp.ones((8, STACK * TOK), jnp.float32)
    sums[1] = jnp.ones((8, STACK * TOK), jnp.float32)
    ones = jnp.ones((16, WINDOW), jnp.bfloat16)
    def one_head(h, stack, with_top):
        lanes = pl.ds(pl.multiple_of((first + h) * HD, HD), HD)
        key_rows = jnp.concatenate([block[0, :, lanes] if len(block.shape) == 3 else block[:, lanes] for block in key_blocks], 0)
        value_rows = jnp.concatenate([block[0, :, lanes] if len(block.shape) == 3 else block[:, lanes] for block in value_blocks], 0)
        value_side = jnp.concatenate([value_rows.T, ones], 0)
        mask = jnp.concatenate([bias[...]] * stack, 1)

        def head_lanes(h, g):
            return pl.ds(pl.multiple_of(h * HEAD_WIDTH + g * HD, HD), HD)

        def score(g0):
            rows = jnp.concatenate([q_buf[:, head_lanes(h, g0 + g)] for g in range(stack)], 0)
            return lax.dot_general(key_rows, rows, NT, preferred_element_type=jnp.float32)

        def finish(g0, scores):
            if with_top:
                masked = scores + mask
                exponent = (masked - jnp.max(masked, axis=0, keepdims=True)) * EXP_SCALE
            else:
                exponent = scores * EXP_SCALE + mask
            weights = jnp.exp2(exponent).astype(jnp.bfloat16)
            mixed = lax.dot_general(value_side, weights, NN, preferred_element_type=jnp.float32)
            if not with_top:
                total = mixed[HD : HD + 8]
                sums[0] = jnp.minimum(sums[0], total)
                sums[1] = jnp.maximum(sums[1], total)
            result = (mixed[:HD] * (1.0 / mixed[HD : HD + 1])).astype(jnp.bfloat16)
            for g in range(stack):
                o_buf[:, head_lanes(h, g0 + g)] = result[:, g * TOK : (g + 1) * TOK].T
            if (g0 + stack) % STACK == 0:
                out_copy(h, g0 + stack - STACK).start()

        scores = score(0)
        for g0 in range(0, GROUP, stack):
            following = score(g0 + stack) if g0 + stack < GROUP else None
            finish(g0, scores)
            scores = following

    def first_pass(h, carry):
        query_copy(h).wait()
        one_head(h, STACK, False)
        return carry

    def wait_out(h, carry):
        for g0 in range(0, GROUP, STACK):
            out_copy(h, g0).wait()
        return carry

    lax.fori_loop(0, heads, first_pass, 0)
    lax.fori_loop(0, heads, wait_out, 0)

    in_range = (jnp.min(sums[0]) > SUM_LEAST) & (jnp.max(sums[1]) < SUM_MOST)

    @pl.when(jnp.logical_not(in_range))
    def _():
        def second_pass(h, carry):
            one_head(h, STACK_TOP, True)
            return wait_out(h, carry)

        lax.fori_loop(0, heads, second_pass, 0)


def attend(first, heads, where, queries, *operands, partial=None):
    more = () if partial is None else (partial,)
    return pl.pallas_call(
        functools.partial(attend_kernel, first, heads),
        in_specs=[SMEM, HBM] + [VMEM] * len(operands) + [HBM] * len(more),
        out_specs=HBM,
        out_shape=jax.ShapeDtypeStruct(queries.shape, jnp.bfloat16),
        scratch_shapes=[
            pltpu.VMEM((TOK, heads * HEAD_WIDTH), jnp.bfloat16),
            pltpu.VMEM((TOK, heads * HEAD_WIDTH), jnp.bfloat16),
            pltpu.VMEM((WINDOW, TOK), jnp.float32),
            pltpu.VMEM((2, 8, STACK * TOK), jnp.float32),
            pltpu.SemaphoreType.DMA((heads,)),
            pltpu.SemaphoreType.DMA((heads,)),
        ],
        input_output_aliases={2 + len(operands): 0} if more else {},
        compiler_params=pltpu.CompilerParams(vmem_limit_bytes=51 * 2**20),
        cost_estimate=CHEAP,
        name=f"attend{first}",
    )(where, queries, *operands, *more)


def body(queries, keys, values, lengths, owners):
    ctx_index = lax.axis_index("ctx")
    ctx_count = lax.axis_size("ctx")
    where = jnp.concatenate([ctx_index.astype(jnp.int32).reshape(1), lengths[0]])

    def chips_on(block, chips):
        step = 2 * chips
        return lax.ppermute(block, "ctx", [(i, (i + step) % ctx_count) for i in range(ctx_count)])

    near_keys, near_values = chips_on(keys, 1), chips_on(values, 1)
    far_keys, far_values = chips_on(keys, 2), chips_on(values, 2)

    message = pack(owners.reshape(PAGES_DEV), keys, values)
    message = message.reshape(KVH * OWNERS, CAP, ROW)
    received = lax.all_to_all(message, ("ctx", "dec"), split_axis=0, concat_axis=0, tiled=True)

    even = ctx_index % 2 == 0
    handed = [
        jnp.where(even, keys, far_keys),
        near_keys,
        jnp.where(even, values, far_values),
        near_values,
    ]
    swapped = lax.ppermute(jnp.concatenate(handed, 0), "ctx", [(i, i ^ 1) for i in range(ctx_count)])
    attended = None
    for first, heads in PARTS:
        attended = attend(
            first,
            heads,
            where,
            queries,
            keys,
            values,
            near_keys,
            near_values,
            far_keys,
            far_values,
            swapped,
            partial=attended,
        )
    attended, received = lax.optimization_barrier((attended, received))
    return (attended,) + unpack(received)


def solution(mesh):
    placed = (
        P("dec", "ctx", None),
        P("dec", "ctx", None),
        P("dec", "ctx", None),
        P("dec", None),
        P("dec", "ctx", None),
    )
    return jax.shard_map(
        body,
        mesh=mesh,
        in_specs=placed,
        out_specs=(
            P("dec", "ctx", None),
            P(None, "ctx", "dec", None),
            P(None, "ctx", "dec", None),
            P(None, "ctx", "dec", None),
            P(None, "ctx", "dec", None),
        ),
        check_vma=False,
    )
```

```python
import functools
import math

import jax
import jax.numpy as jnp
from jax import lax
from jax.experimental import pallas as pl
from jax.experimental.pallas import tpu as pltpu
from jax.sharding import PartitionSpec as P

HD = 128
KVH = 8
GROUP = 16
PAGE = 8
CAP = 2
REQS = 4
TOK = 128
PAGES_DEV = 16
OWNERS = 16
BLOCKS = 5
WINDOW = BLOCKS * TOK
ROW = 2 * PAGE * HD + HD
STACK = 8
STACK_TOP = 4
HEAD_WIDTH = GROUP * HD
SUM_LEAST = 2.0**-100
SUM_MOST = 2.0**100
PARTS = ((0, 8),)
EXP_SCALE = math.log2(math.e) / math.sqrt(HD)
INV_ROOT = 1.0 / math.sqrt(HD)
NT = (((1,), (1,)), ((), ()))
NN = (((1,), (0,)), ((), ()))
CHEAP = pl.CostEstimate(flops=1000, bytes_accessed=1000, transcendentals=0)
ANY = pl.BlockSpec(memory_space=pl.ANY)
HBM = pl.BlockSpec(memory_space=pltpu.HBM)
SMEM = pl.BlockSpec(memory_space=pltpu.SMEM)
VMEM = pl.BlockSpec(memory_space=pltpu.VMEM)


def iota(shape, axis):
    return lax.broadcasted_iota(jnp.int32, shape, axis)


def pack_kernel(owners, keys, values, out):
    row, col = iota((HD, HD), 0), iota((HD, HD), 1)
    common = row & col
    parity = jnp.zeros((HD, HD), jnp.int32)
    for bit in range(7):
        parity = parity + ((common >> bit) & 1)
    signs = (1 - 2 * (parity & 1)).astype(jnp.float32).astype(jnp.bfloat16)
    position = iota((1, TOK), 1)
    page, within = position // PAGE, position % PAGE
    slot = jnp.zeros((1, TOK), jnp.int32)
    for p in range(PAGES_DEV):
        rank = jnp.int32(0)
        for q in range(p):
            rank = rank + (owners[q] == owners[p]).astype(jnp.int32)
        slot = jnp.where(page == p, owners[p] * CAP + rank, slot)
    slots = OWNERS * CAP
    place = iota((PAGE * slots, TOK), 0)
    select = jnp.where((place % slots == slot) & (place // slots == within), 1.0, 0.0).astype(jnp.bfloat16)
    any_row = jnp.where(iota((slots, TOK), 0) == slot, 1.0, 0.0).astype(jnp.bfloat16)
    lane, in_page = iota((TOK, HD), 1), iota((TOK, HD), 0) % PAGE
    for h in range(KVH):
        scales = jnp.zeros((TOK, HD), jnp.float32)
        for which, rows in enumerate((keys, values)):
            rotated = (
                lax.dot_general(rows[0, :, h * HD : (h + 1) * HD], signs, NN, preferred_element_type=jnp.float32)
                * INV_ROOT
            )
            scale = (jnp.max(jnp.abs(rotated), axis=-1, keepdims=True) + 1e-06).astype(jnp.bfloat16)
            scale = scale.astype(jnp.float32)
            codes = (rotated / scale).astype(jnp.bfloat16)
            placed = lax.dot_general(select, codes, NN, preferred_element_type=jnp.float32).astype(jnp.bfloat16)
            for i in range(PAGE):
                at = (which * PAGE + i) * HD
                out[h, :, at : at + HD] = placed[i * slots : (i + 1) * slots]
            scales = jnp.where(lane == which * PAGE + in_page, scale, scales)
        out[h, :, 2 * PAGE * HD :] = lax.dot_general(
            any_row, scales.astype(jnp.bfloat16), NN, preferred_element_type=jnp.float32
        ).astype(jnp.bfloat16)


def pack(owners, keys, values):
    return pl.pallas_call(
        pack_kernel,
        in_specs=[SMEM, VMEM, VMEM],
        out_specs=VMEM,
        out_shape=jax.ShapeDtypeStruct((KVH, OWNERS * CAP, ROW), jnp.bfloat16),
        compiler_params=pltpu.CompilerParams(vmem_limit_bytes=60 * 2**20),
        cost_estimate=CHEAP,
        name="pack",
    )(owners, keys, values)


def unpack_kernel(received, cache_keys, cache_values, key_scales, value_scales, buf, in_sem, out_sem):
    half = PAGE * HD
    spans = ((2 * half, HD), (0, half), (half, half))
    loads = [
        pltpu.make_async_copy(received.at[:, :, pl.ds(at, width)], buf.at[:, :, pl.ds(at, width)], in_sem.at[n])
        for n, (at, width) in enumerate(spans)
    ]
    for load in loads:
        load.start()
    stores = [
        pltpu.make_async_copy(buf.at[:, :, pl.ds(0, half)], cache_keys.at[:, 0], out_sem.at[0]),
        pltpu.make_async_copy(buf.at[:, :, pl.ds(half, half)], cache_values.at[:, 0], out_sem.at[1]),
    ]
    for load, store in zip(loads[1:], stores):
        load.wait()
        store.start()
    loads[0].wait()
    for slot in range(CAP):
        turned = buf[:, slot, 2 * half :].T
        key_scales[slot] = turned[:PAGE]
        value_scales[slot] = turned[PAGE : 2 * PAGE]
    for store in stores:
        store.wait()


def unpack(received):
    sources = received.shape[0]
    cache = jax.ShapeDtypeStruct((sources, 1, CAP, PAGE * HD), jnp.bfloat16)
    scales = jax.ShapeDtypeStruct((CAP, PAGE, sources), jnp.bfloat16)
    cache_keys, cache_values, key_scales, value_scales = pl.pallas_call(
        unpack_kernel,
        in_specs=[ANY],
        out_specs=[HBM, HBM, VMEM, VMEM],
        out_shape=[cache, cache, scales, scales],
        scratch_shapes=[
            pltpu.VMEM(received.shape, jnp.bfloat16),
            pltpu.SemaphoreType.DMA((3,)),
            pltpu.SemaphoreType.DMA((2,)),
        ],
        cost_estimate=CHEAP,
        name="unpack",
    )(received)
    return (
        cache_keys,
        cache_values,
        key_scales.transpose(2, 0, 1)[:, None],
        value_scales.transpose(2, 0, 1)[:, None],
    )


def attend_kernel(first, heads, where, queries, *rest):
    out, q_buf, o_buf, bias, sums, q_sem, o_sem = rest[-7:]
    def query_copy(h):
        at = pl.ds(pl.multiple_of(h * HEAD_WIDTH, HEAD_WIDTH), HEAD_WIDTH)
        from_at = pl.ds(pl.multiple_of((first + h) * HEAD_WIDTH, HEAD_WIDTH), HEAD_WIDTH)
        return pltpu.make_async_copy(queries.at[0, :, from_at], q_buf.at[:, at], q_sem.at[h])

    def out_copy(h, g0):
        width = STACK * HD
        at = pl.ds(pl.multiple_of(h * HEAD_WIDTH + g0 * HD, width), width)
        to_at = pl.ds(pl.multiple_of((first + h) * HEAD_WIDTH + g0 * HD, width), width)
        return pltpu.make_async_copy(o_buf.at[:, at], out.at[0, :, to_at], o_sem.at[h])

    for h in range(heads):
        query_copy(h).start()

    ctx = where[0]
    core = lax.rem(ctx, 2)
    query_pos = ctx * TOK + iota((TOK, TOK), 1)
    start = jnp.zeros((TOK, TOK), jnp.int32)
    end = jnp.int32(0)
    for r in range(REQS):
        end = end + where[1 + r]
        start = jnp.where(query_pos >= end, end, start)
    back = (4, jnp.where(core == 0, 3, 1), 2, jnp.where(core == 0, 1, 3), 0)
    even = jnp.full((TOK, HD), core, jnp.int32) == 0
    for b in range(BLOCKS):
        key_pos = (ctx - back[b]) * TOK + iota((TOK, TOK), 0)
        kept = (key_pos >= start) & (key_pos <= query_pos)
        bias[b * TOK : (b + 1) * TOK, :] = jnp.where(kept, 0.0, -1e30)
    sums[0] = jnp.ones((8, STACK * TOK), jnp.float32)
    sums[1] = jnp.ones((8, STACK * TOK), jnp.float32)
    ones = jnp.ones((16, WINDOW), jnp.bfloat16)
    def window(arrays, lanes):
        own, beside, near, near_beside, far, far_beside = (array[0, :, lanes] for array in arrays)
        third = jnp.where(even, far_beside, beside)
        return jnp.concatenate([far, third, near, near_beside, own], 0)

    def one_head(h, stack, with_top):
        lanes = pl.ds(pl.multiple_of((first + h) * HD, HD), HD)
        key_rows, value_rows = window(rest[0:12:2], lanes), window(rest[1:12:2], lanes)
        value_side = jnp.concatenate([value_rows.T, ones], 0)
        mask = jnp.concatenate([bias[...]] * stack, 1)

        def head_lanes(h, g):
            return pl.ds(pl.multiple_of(h * HEAD_WIDTH + g * HD, HD), HD)

        def score(g0):
            rows = jnp.concatenate([q_buf[:, head_lanes(h, g0 + g)] for g in range(stack)], 0)
            return lax.dot_general(key_rows, rows, NT, preferred_element_type=jnp.float32)

        def finish(g0, scores):
            if with_top:
                masked = scores + mask
                exponent = (masked - jnp.max(masked, axis=0, keepdims=True)) * EXP_SCALE
            else:
                exponent = scores * EXP_SCALE + mask
            weights = jnp.exp2(exponent).astype(jnp.bfloat16)
            mixed = lax.dot_general(value_side, weights, NN, preferred_element_type=jnp.float32)
            if not with_top:
                total = mixed[HD : HD + 8]
                sums[0] = jnp.minimum(sums[0], total)
                sums[1] = jnp.maximum(sums[1], total)
            result = (mixed[:HD] * (1.0 / mixed[HD : HD + 1])).astype(jnp.bfloat16)
            for g in range(stack):
                o_buf[:, head_lanes(h, g0 + g)] = result[:, g * TOK : (g + 1) * TOK].T
            if (g0 + stack) % STACK == 0:
                out_copy(h, g0 + stack - STACK).start()

        scores = score(0)
        for g0 in range(0, GROUP, stack):
            following = score(g0 + stack) if g0 + stack < GROUP else None
            finish(g0, scores)
            scores = following

    def first_pass(h, carry):
        query_copy(h).wait()
        one_head(h, STACK, False)
        return carry

    def wait_out(h, carry):
        for g0 in range(0, GROUP, STACK):
            out_copy(h, g0).wait()
        return carry

    lax.fori_loop(0, heads, first_pass, 0)
    lax.fori_loop(0, heads, wait_out, 0)

    in_range = (jnp.min(sums[0]) > SUM_LEAST) & (jnp.max(sums[1]) < SUM_MOST)

    @pl.when(jnp.logical_not(in_range))
    def _():
        def second_pass(h, carry):
            one_head(h, STACK_TOP, True)
            return wait_out(h, carry)

        lax.fori_loop(0, heads, second_pass, 0)


def attend(first, heads, where, queries, *operands, partial=None):
    more = () if partial is None else (partial,)
    return pl.pallas_call(
        functools.partial(attend_kernel, first, heads),
        in_specs=[SMEM, HBM] + [VMEM] * len(operands) + [HBM] * len(more),
        out_specs=HBM,
        out_shape=jax.ShapeDtypeStruct(queries.shape, jnp.bfloat16),
        scratch_shapes=[
            pltpu.VMEM((TOK, heads * HEAD_WIDTH), jnp.bfloat16),
            pltpu.VMEM((TOK, heads * HEAD_WIDTH), jnp.bfloat16),
            pltpu.VMEM((WINDOW, TOK), jnp.float32),
            pltpu.VMEM((2, 8, STACK * TOK), jnp.float32),
            pltpu.SemaphoreType.DMA((heads,)),
            pltpu.SemaphoreType.DMA((heads,)),
        ],
        input_output_aliases={2 + len(operands): 0} if more else {},
        compiler_params=pltpu.CompilerParams(vmem_limit_bytes=51 * 2**20),
        cost_estimate=pl.CostEstimate(flops=8000000000, bytes_accessed=1000, transcendentals=0),
        name=f"attend{first}",
    )(where, queries, *operands, *more)


def body(queries, keys, values, lengths, owners):
    ctx_index = lax.axis_index("ctx")
    ctx_count = lax.axis_size("ctx")
    where = jnp.concatenate([ctx_index.astype(jnp.int32).reshape(1), lengths[0]])

    def chips_on(block, chips):
        step = 2 * chips
        return lax.ppermute(block, "ctx", [(i, (i + step) % ctx_count) for i in range(ctx_count)])

    def swap(block):
        return lax.ppermute(block, "ctx", [(i, i ^ 1) for i in range(ctx_count)])

    near_values = chips_on(values, 1)
    ahead_keys = chips_on(keys, -1)
    near_keys = chips_on(keys, 1)
    beside = (swap(keys), swap(values))

    message = pack(owners.reshape(PAGES_DEV), keys, values)
    message = message.reshape(KVH * OWNERS, CAP, ROW)
    near_values, ahead_keys, beside, message = lax.optimization_barrier(
        (near_values, ahead_keys, beside, message)
    )
    far_values = chips_on(near_values, 1)
    far_keys = chips_on(ahead_keys, -1)
    received = lax.all_to_all(message, ("ctx", "dec"), split_axis=0, concat_axis=0, tiled=True)

    near = (near_keys, near_values)
    far = (far_keys, far_values)
    near_beside = (swap(near_keys), swap(near_values))
    far_beside = (swap(far_keys), swap(far_values))
    attended = None
    for first, heads in PARTS:
        attended = attend(
            first, heads, where, queries, keys, values, *beside, *near, *near_beside, *far, *far_beside, partial=attended
        )
    attended, received = lax.optimization_barrier((attended, received))
    return (attended,) + unpack(received)


def solution(mesh):
    placed = (
        P("dec", "ctx", None),
        P("dec", "ctx", None),
        P("dec", "ctx", None),
        P("dec", None),
        P("dec", "ctx", None),
    )
    return jax.shard_map(
        body,
        mesh=mesh,
        in_specs=placed,
        out_specs=(
            P("dec", "ctx", None),
            P(None, "ctx", "dec", None),
            P(None, "ctx", "dec", None),
            P(None, "ctx", "dec", None),
            P(None, "ctx", "dec", None),
        ),
        check_vma=False,
    )
```

```python
import functools
import math

import jax
import jax.numpy as jnp
from jax import lax
from jax.experimental import pallas as pl
from jax.experimental.pallas import tpu as pltpu
from jax.sharding import PartitionSpec as P

HD = 128
KVH = 8
GROUP = 16
PAGE = 8
CAP = 2
REQS = 4
TOK = 128
PAGES_DEV = 16
OWNERS = 16
BLOCKS = 5
WINDOW = BLOCKS * TOK
ROW = 2 * PAGE * HD + HD
STACK = 8
STACK_TOP = 4
HEAD_WIDTH = GROUP * HD
SUM_LEAST = 2.0**-100
SUM_MOST = 2.0**100
PARTS = ((0, 8),)
EXP_SCALE = math.log2(math.e) / math.sqrt(HD)
INV_ROOT = 1.0 / math.sqrt(HD)
NT = (((1,), (1,)), ((), ()))
NN = (((1,), (0,)), ((), ()))
CHEAP = pl.CostEstimate(flops=1000, bytes_accessed=1000, transcendentals=0)
HBM = pl.BlockSpec(memory_space=pltpu.HBM)
SMEM = pl.BlockSpec(memory_space=pltpu.SMEM)
VMEM = pl.BlockSpec(memory_space=pltpu.VMEM)


def iota(shape, axis):
    return lax.broadcasted_iota(jnp.int32, shape, axis)


def pack_kernel(owners, keys, values, out, held, sem):
    row, col = iota((HD, HD), 0), iota((HD, HD), 1)
    common = row & col
    parity = jnp.zeros((HD, HD), jnp.int32)
    for bit in range(7):
        parity = parity + ((common >> bit) & 1)
    signs = (1 - 2 * (parity & 1)).astype(jnp.float32).astype(jnp.bfloat16)
    position = iota((1, TOK), 1)
    page, within = position // PAGE, position % PAGE
    slot = jnp.zeros((1, TOK), jnp.int32)
    for p in range(PAGES_DEV):
        rank = jnp.int32(0)
        for q in range(p):
            rank = rank + (owners[q] == owners[p]).astype(jnp.int32)
        slot = jnp.where(page == p, owners[p] * CAP + rank, slot)
    slots = OWNERS * CAP
    place = iota((PAGE * slots, TOK), 0)
    select = jnp.where((place % slots == slot) & (place // slots == within), 1.0, 0.0).astype(jnp.bfloat16)
    any_row = jnp.where(iota((slots, TOK), 0) == slot, 1.0, 0.0).astype(jnp.bfloat16)
    lane, in_page = iota((TOK, HD), 1), iota((TOK, HD), 0) % PAGE
    def put(h, at, tile):
        held[h * OWNERS : (h + 1) * OWNERS, :, at : at + HD] = tile.reshape(OWNERS, CAP, HD).astype(jnp.bfloat16)

    def head_copy(h):
        rows = pl.ds(h * OWNERS, OWNERS)
        return pltpu.make_async_copy(held.at[rows], out.at[rows], sem.at[h])

    for h in range(KVH):
        scales = jnp.zeros((TOK, HD), jnp.float32)
        codes = []
        for which, rows in enumerate((keys, values)):
            rotated = (
                lax.dot_general(rows[0, :, h * HD : (h + 1) * HD], signs, NN, preferred_element_type=jnp.float32)
                * INV_ROOT
            )
            scale = (jnp.max(jnp.abs(rotated), axis=-1, keepdims=True) + 1e-06).astype(jnp.bfloat16)
            scale = scale.astype(jnp.float32)
            codes.append((rotated * (1.0 / scale)).astype(jnp.bfloat16))
            scales = jnp.where(lane == which * PAGE + in_page, scale, scales)
        placed = lax.dot_general(select, jnp.concatenate(codes, 1), NN, preferred_element_type=jnp.float32)
        for which in range(2):
            for i in range(PAGE):
                put(h, (which * PAGE + i) * HD, placed[i * slots : (i + 1) * slots, which * HD : (which + 1) * HD])
        scales = lax.dot_general(any_row, scales.astype(jnp.bfloat16), NN, preferred_element_type=jnp.float32)
        put(h, 2 * PAGE * HD, scales)
        head_copy(h).start()
    for h in range(KVH):
        head_copy(h).wait()


def pack(owners, keys, values):
    shape = (KVH * OWNERS, CAP, ROW)
    return pl.pallas_call(
        pack_kernel,
        in_specs=[SMEM, VMEM, VMEM],
        out_specs=HBM,
        out_shape=jax.ShapeDtypeStruct(shape, jnp.bfloat16),
        scratch_shapes=[pltpu.VMEM(shape, jnp.bfloat16), pltpu.SemaphoreType.DMA((KVH,))],
        compiler_params=pltpu.CompilerParams(vmem_limit_bytes=60 * 2**20),
        cost_estimate=CHEAP,
        name="pack",
    )(owners, keys, values)


def unpack_kernel(received, cache_keys, cache_values, key_scales, value_scales, sem):
    half = PAGE * HD
    copies = [
        pltpu.make_async_copy(received.at[:, :, pl.ds(0, half)], cache_keys.at[:, 0], sem.at[0]),
        pltpu.make_async_copy(received.at[:, :, pl.ds(half, half)], cache_values.at[:, 0], sem.at[1]),
    ]
    for copy in copies:
        copy.start()
    for slot in range(CAP):
        turned = received[:, slot, 2 * half :].T
        key_scales[slot] = turned[:PAGE]
        value_scales[slot] = turned[PAGE : 2 * PAGE]
    for copy in copies:
        copy.wait()


def unpack(received):
    sources = received.shape[0]
    cache = jax.ShapeDtypeStruct((sources, 1, CAP, PAGE * HD), jnp.bfloat16)
    scales = jax.ShapeDtypeStruct((CAP, PAGE, sources), jnp.bfloat16)
    cache_keys, cache_values, key_scales, value_scales = pl.pallas_call(
        unpack_kernel,
        in_specs=[VMEM],
        out_specs=[HBM, HBM, VMEM, VMEM],
        out_shape=[cache, cache, scales, scales],
        scratch_shapes=[pltpu.SemaphoreType.DMA((2,))],
        compiler_params=pltpu.CompilerParams(vmem_limit_bytes=8 * 2**20),
        cost_estimate=CHEAP,
        name="unpack",
    )(received)
    return (
        cache_keys,
        cache_values,
        key_scales.transpose(2, 0, 1)[:, None],
        value_scales.transpose(2, 0, 1)[:, None],
    )


def mask_kernel(lengths, bias):
    ctx = lax.axis_index("ctx")
    core = lax.rem(ctx, 2)
    query_pos = ctx * TOK + iota((TOK, TOK), 1)
    start = jnp.zeros((TOK, TOK), jnp.int32)
    end = jnp.int32(0)
    for r in range(REQS):
        end = end + lengths[0, r]
        start = jnp.where(query_pos >= end, end, start)
    back = (4, jnp.where(core == 0, 3, 1), 2, jnp.where(core == 0, 1, 3), 0)
    for b in range(BLOCKS):
        key_pos = (ctx - back[b]) * TOK + iota((TOK, TOK), 0)
        kept = (key_pos >= start) & (key_pos <= query_pos)
        bias[b * TOK : (b + 1) * TOK, :] = jnp.where(kept, 0.0, -1e30)


def mask(lengths):
    return pl.pallas_call(
        mask_kernel,
        in_specs=[SMEM],
        out_specs=VMEM,
        out_shape=jax.ShapeDtypeStruct((WINDOW, TOK), jnp.float32),
        cost_estimate=pl.CostEstimate(flops=2000000000, bytes_accessed=1000, transcendentals=0),
        compiler_params=pltpu.CompilerParams(vmem_limit_bytes=8 * 2**20),
        name="mask",
    )(lengths)


def attend_kernel(first, heads, bias, queries, *rest):
    out, o_buf, sums, o_sem = rest[-4:]
    def out_copy(h, g0):
        width = STACK * HD
        at = pl.ds(pl.multiple_of(h * HEAD_WIDTH + g0 * HD, width), width)
        to_at = pl.ds(pl.multiple_of((first + h) * HEAD_WIDTH + g0 * HD, width), width)
        return pltpu.make_async_copy(o_buf.at[:, at], out.at[0, :, to_at], o_sem.at[h])

    even = jnp.full((TOK, HD), lax.rem(lax.axis_index("ctx"), 2), jnp.int32) == 0
    sums[0] = jnp.ones((8, STACK * TOK), jnp.float32)
    sums[1] = jnp.ones((8, STACK * TOK), jnp.float32)
    ones = jnp.ones((16, WINDOW), jnp.bfloat16)
    def window(arrays, lanes):
        own, beside, near, near_beside, far, far_beside = (array[0, :, lanes] for array in arrays)
        third = jnp.where(even, far_beside, beside)
        return jnp.concatenate([far, third, near, near_beside, own], 0)

    def one_head(h, stack, with_top):
        lanes = pl.ds(pl.multiple_of((first + h) * HD, HD), HD)
        key_rows, value_rows = window(rest[0:12:2], lanes), window(rest[1:12:2], lanes)
        value_side = jnp.concatenate([value_rows.T, ones], 0)
        mask = jnp.concatenate([bias[...]] * stack, 1)

        def head_lanes(h, g):
            return pl.ds(pl.multiple_of(h * HEAD_WIDTH + g * HD, HD), HD)

        def score(g0):
            rows = jnp.concatenate([queries[0, :, head_lanes(first + h, g0 + g)] for g in range(stack)], 0)
            return lax.dot_general(key_rows, rows, NT, preferred_element_type=jnp.float32)

        def finish(g0, scores):
            if with_top:
                masked = scores + mask
                exponent = (masked - jnp.max(masked, axis=0, keepdims=True)) * EXP_SCALE
            else:
                exponent = scores * EXP_SCALE + mask
            weights = jnp.exp2(exponent).astype(jnp.bfloat16)
            mixed = lax.dot_general(value_side, weights, NN, preferred_element_type=jnp.float32)
            if not with_top:
                total = mixed[HD : HD + 8]
                sums[0] = jnp.minimum(sums[0], total)
                sums[1] = jnp.maximum(sums[1], total)
            result = (mixed[:HD] * (1.0 / mixed[HD : HD + 1])).astype(jnp.bfloat16)
            for g in range(stack):
                o_buf[:, head_lanes(h, g0 + g)] = result[:, g * TOK : (g + 1) * TOK].T
            if (g0 + stack) % STACK == 0:
                out_copy(h, g0 + stack - STACK).start()

        scores = score(0)
        for g0 in range(0, GROUP, stack):
            following = score(g0 + stack) if g0 + stack < GROUP else None
            finish(g0, scores)
            scores = following

    def first_pass(h, carry):
        one_head(h, STACK, False)
        return carry

    def wait_out(h, carry):
        for g0 in range(0, GROUP, STACK):
            out_copy(h, g0).wait()
        return carry

    lax.fori_loop(0, heads, first_pass, 0)
    lax.fori_loop(0, heads, wait_out, 0)

    in_range = (jnp.min(sums[0]) > SUM_LEAST) & (jnp.max(sums[1]) < SUM_MOST)

    @pl.when(jnp.logical_not(in_range))
    def _():
        def second_pass(h, carry):
            one_head(h, STACK_TOP, True)
            return wait_out(h, carry)

        lax.fori_loop(0, heads, second_pass, 0)


def attend(first, heads, bias, queries, *operands, partial=None):
    more = () if partial is None else (partial,)
    return pl.pallas_call(
        functools.partial(attend_kernel, first, heads),
        in_specs=[VMEM, VMEM] + [VMEM] * len(operands) + [HBM] * len(more),
        out_specs=HBM,
        out_shape=jax.ShapeDtypeStruct(queries.shape, jnp.bfloat16),
        scratch_shapes=[
            pltpu.VMEM((TOK, heads * HEAD_WIDTH), jnp.bfloat16),
            pltpu.VMEM((2, 8, STACK * TOK), jnp.float32),
            pltpu.SemaphoreType.DMA((heads,)),
        ],
        input_output_aliases={2 + len(operands): 0} if more else {},
        compiler_params=pltpu.CompilerParams(vmem_limit_bytes=28 * 2**20),
        cost_estimate=pl.CostEstimate(flops=6000000000, bytes_accessed=1000, transcendentals=0),
        name=f"attend{first}",
    )(bias, queries, *operands, *more)


def body(queries, keys, values, lengths, owners):
    ctx_count = lax.axis_size("ctx")

    def chips_on(block, chips):
        step = 2 * chips
        return lax.ppermute(block, "ctx", [(i, (i + step) % ctx_count) for i in range(ctx_count)])

    def swap(block):
        return lax.ppermute(block, "ctx", [(i, i ^ 1) for i in range(ctx_count)])

    near_values = chips_on(values, 1)
    ahead_keys = chips_on(keys, -1)
    near_keys = chips_on(keys, 1)

    message = pack(owners.reshape(PAGES_DEV), keys, values)
    near_values, ahead_keys, message = lax.optimization_barrier((near_values, ahead_keys, message))
    lengths, message = lax.optimization_barrier((lengths, message))
    bias = mask(lengths)
    far_values = chips_on(near_values, 1)
    far_keys = chips_on(ahead_keys, -1)
    received = lax.all_to_all(message, ("ctx", "dec"), split_axis=0, concat_axis=0, tiled=True)

    near_keys, near_values, far_keys, far_values, own = lax.optimization_barrier(
        (near_keys, near_values, far_keys, far_values, (keys, values))
    )
    beside = (swap(own[0]), swap(own[1]))
    near = (near_keys, near_values)
    far = (far_keys, far_values)
    near_beside = (swap(near_keys), swap(near_values))
    far_beside = (swap(far_keys), swap(far_values))
    attended = None
    for first, heads in PARTS:
        attended = attend(
            first, heads, bias, queries, keys, values, *beside, *near, *near_beside, *far, *far_beside, partial=attended
        )
    attended, received = lax.optimization_barrier((attended, received))
    return (attended,) + unpack(received)


def solution(mesh):
    placed = (
        P("dec", "ctx", None),
        P("dec", "ctx", None),
        P("dec", "ctx", None),
        P("dec", None),
        P("dec", "ctx", None),
    )
    return jax.shard_map(
        body,
        mesh=mesh,
        in_specs=placed,
        out_specs=(
            P("dec", "ctx", None),
            P(None, "ctx", "dec", None),
            P(None, "ctx", "dec", None),
            P(None, "ctx", "dec", None),
            P(None, "ctx", "dec", None),
        ),
        check_vma=False,
    )
```

```python
import functools
import math

import jax
import jax.numpy as jnp
from jax import lax
from jax.experimental import pallas as pl
from jax.experimental.pallas import tpu as pltpu
from jax.sharding import PartitionSpec as P

HD = 128
KVH = 8
GROUP = 16
PAGE = 8
CAP = 2
REQS = 4
TOK = 128
PAGES_DEV = 16
OWNERS = 16
BLOCKS = 5
WINDOW = BLOCKS * TOK
ROW = 2 * PAGE * HD + HD
STACK = 8
STACK_TOP = 4
HEAD_WIDTH = GROUP * HD
SUM_LEAST = 2.0**-100
SUM_MOST = 2.0**100
PARTS = ((0, 8),)
EXP_SCALE = math.log2(math.e) / math.sqrt(HD)
INV_ROOT = 1.0 / math.sqrt(HD)
NT = (((1,), (1,)), ((), ()))
NN = (((1,), (0,)), ((), ()))
CHEAP = pl.CostEstimate(flops=1000, bytes_accessed=1000, transcendentals=0)
HBM = pl.BlockSpec(memory_space=pltpu.HBM)
SMEM = pl.BlockSpec(memory_space=pltpu.SMEM)
VMEM = pl.BlockSpec(memory_space=pltpu.VMEM)


def iota(shape, axis):
    return lax.broadcasted_iota(jnp.int32, shape, axis)


def pack_kernel(owners, keys, values, out, held, sem):
    row, col = iota((HD, HD), 0), iota((HD, HD), 1)
    common = row & col
    parity = jnp.zeros((HD, HD), jnp.int32)
    for bit in range(7):
        parity = parity + ((common >> bit) & 1)
    signs = (1 - 2 * (parity & 1)).astype(jnp.float32).astype(jnp.bfloat16)
    position = iota((1, TOK), 1)
    page, within = position // PAGE, position % PAGE
    slot = jnp.zeros((1, TOK), jnp.int32)
    for p in range(PAGES_DEV):
        rank = jnp.int32(0)
        for q in range(p):
            rank = rank + (owners[q] == owners[p]).astype(jnp.int32)
        slot = jnp.where(page == p, owners[p] * CAP + rank, slot)
    slots = OWNERS * CAP
    place = iota((PAGE * slots, TOK), 0)
    select = jnp.where((place % slots == slot) & (place // slots == within), 1.0, 0.0).astype(jnp.bfloat16)
    any_row = jnp.where(iota((slots, TOK), 0) == slot, 1.0, 0.0).astype(jnp.bfloat16)
    lane, in_page = iota((TOK, HD), 1), iota((TOK, HD), 0) % PAGE
    def put(h, at, tile):
        held[h * OWNERS : (h + 1) * OWNERS, :, at : at + HD] = tile.reshape(OWNERS, CAP, HD).astype(jnp.bfloat16)

    def head_copy(h):
        rows = pl.ds(h * OWNERS, OWNERS)
        return pltpu.make_async_copy(held.at[rows], out.at[rows], sem.at[h])

    for h in range(KVH):
        scales = jnp.zeros((TOK, HD), jnp.float32)
        codes = []
        for which, rows in enumerate((keys, values)):
            rotated = (
                lax.dot_general(rows[0, :, h * HD : (h + 1) * HD], signs, NN, preferred_element_type=jnp.float32)
                * INV_ROOT
            )
            scale = (jnp.max(jnp.abs(rotated), axis=-1, keepdims=True) + 1e-06).astype(jnp.bfloat16)
            scale = scale.astype(jnp.float32)
            codes.append((rotated * (1.0 / scale)).astype(jnp.bfloat16))
            scales = jnp.where(lane == which * PAGE + in_page, scale, scales)
        placed = lax.dot_general(select, jnp.concatenate(codes, 1), NN, preferred_element_type=jnp.float32)
        for which in range(2):
            for i in range(PAGE):
                put(h, (which * PAGE + i) * HD, placed[i * slots : (i + 1) * slots, which * HD : (which + 1) * HD])
        scales = lax.dot_general(any_row, scales.astype(jnp.bfloat16), NN, preferred_element_type=jnp.float32)
        put(h, 2 * PAGE * HD, scales)
        head_copy(h).start()
    for h in range(KVH):
        head_copy(h).wait()


def pack(owners, keys, values):
    shape = (KVH * OWNERS, CAP, ROW)
    return pl.pallas_call(
        pack_kernel,
        in_specs=[SMEM, VMEM, VMEM],
        out_specs=HBM,
        out_shape=jax.ShapeDtypeStruct(shape, jnp.bfloat16),
        scratch_shapes=[pltpu.VMEM(shape, jnp.bfloat16), pltpu.SemaphoreType.DMA((KVH,))],
        compiler_params=pltpu.CompilerParams(vmem_limit_bytes=60 * 2**20),
        cost_estimate=CHEAP,
        name="pack",
    )(owners, keys, values)


def unpack_kernel(received, cache_keys, cache_values, key_scales, value_scales, held, sem):
    half = PAGE * HD
    copies = [
        pltpu.make_async_copy(received.at[:, :, pl.ds(0, half)], cache_keys.at[:, 0], sem.at[0]),
        pltpu.make_async_copy(received.at[:, :, pl.ds(half, half)], cache_values.at[:, 0], sem.at[1]),
        pltpu.make_async_copy(held.at[0], key_scales, sem.at[2]),
        pltpu.make_async_copy(held.at[1], value_scales, sem.at[3]),
    ]
    copies[0].start()
    copies[1].start()
    for slot in range(CAP):
        turned = received[:, slot, 2 * half :].T
        held[0, slot] = turned[:PAGE]
        held[1, slot] = turned[PAGE : 2 * PAGE]
    copies[2].start()
    copies[3].start()
    for copy in copies:
        copy.wait()


def unpack(received):
    sources = received.shape[0]
    cache = jax.ShapeDtypeStruct((sources, 1, CAP, PAGE * HD), jnp.bfloat16)
    scales = jax.ShapeDtypeStruct((CAP, PAGE, sources), jnp.bfloat16)
    cache_keys, cache_values, key_scales, value_scales = pl.pallas_call(
        unpack_kernel,
        in_specs=[VMEM],
        out_specs=[HBM] * 4,
        out_shape=[cache, cache, scales, scales],
        scratch_shapes=[pltpu.VMEM((2, CAP, PAGE, sources), jnp.bfloat16), pltpu.SemaphoreType.DMA((4,))],
        compiler_params=pltpu.CompilerParams(vmem_limit_bytes=8 * 2**20),
        cost_estimate=CHEAP,
        name="unpack",
    )(received)
    return (
        cache_keys,
        cache_values,
        key_scales.transpose(2, 0, 1)[:, None],
        value_scales.transpose(2, 0, 1)[:, None],
    )


def mask_kernel(lengths, bias):
    ctx = lax.axis_index("ctx")
    core = lax.rem(ctx, 2)
    query_pos = ctx * TOK + iota((TOK, TOK), 1)
    start = jnp.zeros((TOK, TOK), jnp.int32)
    end = jnp.int32(0)
    for r in range(REQS):
        end = end + lengths[0, r]
        start = jnp.where(query_pos >= end, end, start)
    back = (4, jnp.where(core == 0, 3, 1), 2, jnp.where(core == 0, 1, 3), 0)
    for b in range(BLOCKS):
        key_pos = (ctx - back[b]) * TOK + iota((TOK, TOK), 0)
        kept = (key_pos >= start) & (key_pos <= query_pos)
        bias[b * TOK : (b + 1) * TOK, :] = jnp.where(kept, 0.0, -1e30)


def mask(lengths):
    return pl.pallas_call(
        mask_kernel,
        in_specs=[SMEM],
        out_specs=VMEM,
        out_shape=jax.ShapeDtypeStruct((WINDOW, TOK), jnp.float32),
        cost_estimate=pl.CostEstimate(flops=2000000000, bytes_accessed=1000, transcendentals=0),
        compiler_params=pltpu.CompilerParams(vmem_limit_bytes=8 * 2**20),
        name="mask",
    )(lengths)


def attend_kernel(first, heads, bias, queries, *rest):
    out, o_buf, sums, o_sem = rest[-4:]
    def out_copy(h, g0):
        width = STACK * HD
        at = pl.ds(pl.multiple_of(h * HEAD_WIDTH + g0 * HD, width), width)
        to_at = pl.ds(pl.multiple_of((first + h) * HEAD_WIDTH + g0 * HD, width), width)
        return pltpu.make_async_copy(o_buf.at[:, at], out.at[0, :, to_at], o_sem.at[h])

    even = jnp.full((TOK, HD), lax.rem(lax.axis_index("ctx"), 2), jnp.int32) == 0
    sums[0] = jnp.ones((8, STACK * TOK), jnp.float32)
    sums[1] = jnp.ones((8, STACK * TOK), jnp.float32)
    ones = jnp.ones((16, WINDOW), jnp.bfloat16)
    def window(arrays, lanes):
        own, beside, near, near_beside, far, far_beside = (array[0, :, lanes] for array in arrays)
        third = jnp.where(even, far_beside, beside)
        return jnp.concatenate([far, third, near, near_beside, own], 0)

    def one_head(h, stack, with_top):
        lanes = pl.ds(pl.multiple_of((first + h) * HD, HD), HD)
        key_rows, value_rows = window(rest[0:12:2], lanes), window(rest[1:12:2], lanes)
        value_side = jnp.concatenate([value_rows.T, ones], 0)
        mask = jnp.concatenate([bias[...]] * stack, 1)

        def head_lanes(h, g):
            return pl.ds(pl.multiple_of(h * HEAD_WIDTH + g * HD, HD), HD)

        def score(g0):
            rows = jnp.concatenate([queries[0, :, head_lanes(first + h, g0 + g)] for g in range(stack)], 0)
            return lax.dot_general(key_rows, rows, NT, preferred_element_type=jnp.float32)

        def finish(g0, scores):
            if with_top:
                masked = scores + mask
                exponent = (masked - jnp.max(masked, axis=0, keepdims=True)) * EXP_SCALE
            else:
                exponent = scores * EXP_SCALE + mask
            weights = jnp.exp2(exponent).astype(jnp.bfloat16)
            mixed = lax.dot_general(value_side, weights, NN, preferred_element_type=jnp.float32)
            if not with_top:
                total = mixed[HD : HD + 8]
                sums[0] = jnp.minimum(sums[0], total)
                sums[1] = jnp.maximum(sums[1], total)
            result = (mixed[:HD] * (1.0 / mixed[HD : HD + 1])).astype(jnp.bfloat16)
            for g in range(stack):
                o_buf[:, head_lanes(h, g0 + g)] = result[:, g * TOK : (g + 1) * TOK].T
            if (g0 + stack) % STACK == 0:
                out_copy(h, g0 + stack - STACK).start()

        scores = score(0)
        for g0 in range(0, GROUP, stack):
            following = score(g0 + stack) if g0 + stack < GROUP else None
            finish(g0, scores)
            scores = following

    def first_pass(h, carry):
        one_head(h, STACK, False)
        return carry

    def wait_out(h, carry):
        for g0 in range(0, GROUP, STACK):
            out_copy(h, g0).wait()
        return carry

    lax.fori_loop(0, heads, first_pass, 0)
    lax.fori_loop(0, heads, wait_out, 0)

    in_range = (jnp.min(sums[0]) > SUM_LEAST) & (jnp.max(sums[1]) < SUM_MOST)

    @pl.when(jnp.logical_not(in_range))
    def _():
        def second_pass(h, carry):
            one_head(h, STACK_TOP, True)
            return wait_out(h, carry)

        lax.fori_loop(0, heads, second_pass, 0)


def attend(first, heads, bias, queries, *operands, partial=None):
    more = () if partial is None else (partial,)
    return pl.pallas_call(
        functools.partial(attend_kernel, first, heads),
        in_specs=[VMEM, VMEM] + [VMEM] * len(operands) + [HBM] * len(more),
        out_specs=HBM,
        out_shape=jax.ShapeDtypeStruct(queries.shape, jnp.bfloat16),
        scratch_shapes=[
            pltpu.VMEM((TOK, heads * HEAD_WIDTH), jnp.bfloat16),
            pltpu.VMEM((2, 8, STACK * TOK), jnp.float32),
            pltpu.SemaphoreType.DMA((heads,)),
        ],
        input_output_aliases={2 + len(operands): 0} if more else {},
        compiler_params=pltpu.CompilerParams(vmem_limit_bytes=28 * 2**20),
        cost_estimate=pl.CostEstimate(flops=6000000000, bytes_accessed=1000, transcendentals=0),
        name=f"attend{first}",
    )(bias, queries, *operands, *more)


def body(queries, keys, values, lengths, owners):
    ctx_count = lax.axis_size("ctx")

    def chips_on(block, chips):
        step = 2 * chips
        return lax.ppermute(block, "ctx", [(i, (i + step) % ctx_count) for i in range(ctx_count)])

    def swap(block):
        return lax.ppermute(block, "ctx", [(i, i ^ 1) for i in range(ctx_count)])

    near_values = chips_on(values, 1)
    ahead_keys = chips_on(keys, -1)
    near_keys = chips_on(keys, 1)

    message = pack(owners.reshape(PAGES_DEV), keys, values)
    near_values, ahead_keys, message = lax.optimization_barrier((near_values, ahead_keys, message))
    lengths, message = lax.optimization_barrier((lengths, message))
    bias = mask(lengths)
    far_values = chips_on(near_values, 1)
    far_keys = chips_on(ahead_keys, -1)
    received = lax.all_to_all(message, ("ctx", "dec"), split_axis=0, concat_axis=0, tiled=True)

    near_keys, near_values, far_keys, far_values, own = lax.optimization_barrier(
        (near_keys, near_values, far_keys, far_values, (keys, values))
    )
    beside = (swap(own[0]), swap(own[1]))
    near = (near_keys, near_values)
    far = (far_keys, far_values)
    near_beside = (swap(near_keys), swap(near_values))
    far_beside = (swap(far_keys), swap(far_values))
    attended = None
    for first, heads in PARTS:
        attended = attend(
            first, heads, bias, queries, keys, values, *beside, *near, *near_beside, *far, *far_beside, partial=attended
        )
    attended, received = lax.optimization_barrier((attended, received))
    return (attended,) + unpack(received)


def solution(mesh):
    placed = (
        P("dec", "ctx", None),
        P("dec", "ctx", None),
        P("dec", "ctx", None),
        P("dec", None),
        P("dec", "ctx", None),
    )
    return jax.shard_map(
        body,
        mesh=mesh,
        in_specs=placed,
        out_specs=(
            P("dec", "ctx", None),
            P(None, "ctx", "dec", None),
            P(None, "ctx", "dec", None),
            P(None, "ctx", "dec", None),
            P(None, "ctx", "dec", None),
        ),
        check_vma=False,
    )
```

```python
import functools
import math

import jax
import jax.numpy as jnp
from jax import lax
from jax.experimental import pallas as pl
from jax.experimental.pallas import tpu as pltpu
from jax.sharding import PartitionSpec as P

HD = 128
KVH = 8
GROUP = 16
PAGE = 8
CAP = 2
REQS = 4
TOK = 128
PAGES_DEV = 16
OWNERS = 16
BLOCKS = 5
WINDOW = BLOCKS * TOK
ROW = 2 * PAGE * HD + HD
STACK = 8
STACK_TOP = 4
HEAD_WIDTH = GROUP * HD
SUM_LEAST = 2.0**-100
SUM_MOST = 2.0**100
PARTS = ((0, 8),)
EXP_SCALE = math.log2(math.e) / math.sqrt(HD)
INV_ROOT = 1.0 / math.sqrt(HD)
NT = (((1,), (1,)), ((), ()))
NN = (((1,), (0,)), ((), ()))
CHEAP = pl.CostEstimate(flops=1000, bytes_accessed=1000, transcendentals=0)
HBM = pl.BlockSpec(memory_space=pltpu.HBM)
SMEM = pl.BlockSpec(memory_space=pltpu.SMEM)
VMEM = pl.BlockSpec(memory_space=pltpu.VMEM)


def iota(shape, axis):
    return lax.broadcasted_iota(jnp.int32, shape, axis)


def pack_kernel(owners, keys, values, out, held, sem):
    row, col = iota((HD, HD), 0), iota((HD, HD), 1)
    common = row & col
    parity = jnp.zeros((HD, HD), jnp.int32)
    for bit in range(7):
        parity = parity + ((common >> bit) & 1)
    signs = (1 - 2 * (parity & 1)).astype(jnp.float32).astype(jnp.bfloat16)
    position = iota((1, TOK), 1)
    page, within = position // PAGE, position % PAGE
    slot = jnp.zeros((1, TOK), jnp.int32)
    for p in range(PAGES_DEV):
        rank = jnp.int32(0)
        for q in range(p):
            rank = rank + (owners[q] == owners[p]).astype(jnp.int32)
        slot = jnp.where(page == p, owners[p] * CAP + rank, slot)
    slots = OWNERS * CAP
    place = iota((PAGE * slots, TOK), 0)
    select = jnp.where((place % slots == slot) & (place // slots == within), 1.0, 0.0).astype(jnp.bfloat16)
    any_row = jnp.where(iota((slots, TOK), 0) == slot, 1.0, 0.0).astype(jnp.bfloat16)
    lane, in_page = iota((TOK, HD), 1), iota((TOK, HD), 0) % PAGE
    def put(h, at, tile):
        held[h * OWNERS : (h + 1) * OWNERS, :, at : at + HD] = tile.reshape(OWNERS, CAP, HD).astype(jnp.bfloat16)

    def head_copy(h):
        rows = pl.ds(h * OWNERS, OWNERS)
        return pltpu.make_async_copy(held.at[rows], out.at[rows], sem.at[h])

    for h in range(KVH):
        scales = jnp.zeros((TOK, HD), jnp.float32)
        codes = []
        for which, rows in enumerate((keys, values)):
            rotated = (
                lax.dot_general(rows[0, :, h * HD : (h + 1) * HD], signs, NN, preferred_element_type=jnp.float32)
                * INV_ROOT
            )
            scale = (jnp.max(jnp.abs(rotated), axis=-1, keepdims=True) + 1e-06).astype(jnp.bfloat16)
            scale = scale.astype(jnp.float32)
            codes.append((rotated * (1.0 / scale)).astype(jnp.bfloat16))
            scales = jnp.where(lane == which * PAGE + in_page, scale, scales)
        placed = lax.dot_general(select, jnp.concatenate(codes, 1), NN, preferred_element_type=jnp.float32)
        for which in range(2):
            for i in range(PAGE):
                put(h, (which * PAGE + i) * HD, placed[i * slots : (i + 1) * slots, which * HD : (which + 1) * HD])
        scales = lax.dot_general(any_row, scales.astype(jnp.bfloat16), NN, preferred_element_type=jnp.float32)
        put(h, 2 * PAGE * HD, scales)
        head_copy(h).start()
    for h in range(KVH):
        head_copy(h).wait()


def pack(owners, keys, values):
    shape = (KVH * OWNERS, CAP, ROW)
    return pl.pallas_call(
        pack_kernel,
        in_specs=[SMEM, VMEM, VMEM],
        out_specs=HBM,
        out_shape=jax.ShapeDtypeStruct(shape, jnp.bfloat16),
        scratch_shapes=[pltpu.VMEM(shape, jnp.bfloat16), pltpu.SemaphoreType.DMA((KVH,))],
        compiler_params=pltpu.CompilerParams(vmem_limit_bytes=60 * 2**20),
        cost_estimate=CHEAP,
        name="pack",
    )(owners, keys, values)


def unpack_kernel(received, cache_keys, cache_values, key_scales, value_scales, held, sem):
    half = PAGE * HD
    copies = [
        pltpu.make_async_copy(received.at[:, :, pl.ds(0, half)], cache_keys.at[:, 0], sem.at[0]),
        pltpu.make_async_copy(received.at[:, :, pl.ds(half, half)], cache_values.at[:, 0], sem.at[1]),
        pltpu.make_async_copy(held.at[0], key_scales, sem.at[2]),
        pltpu.make_async_copy(held.at[1], value_scales, sem.at[3]),
    ]
    copies[0].start()
    copies[1].start()
    for slot in range(CAP):
        turned = received[:, slot, 2 * half :].T
        held[0, slot] = turned[:PAGE]
        held[1, slot] = turned[PAGE : 2 * PAGE]
    copies[2].start()
    copies[3].start()
    for copy in copies:
        copy.wait()


def unpack(received):
    sources = received.shape[0]
    cache = jax.ShapeDtypeStruct((sources, 1, CAP, PAGE * HD), jnp.bfloat16)
    scales = jax.ShapeDtypeStruct((CAP, PAGE, sources), jnp.bfloat16)
    cache_keys, cache_values, key_scales, value_scales = pl.pallas_call(
        unpack_kernel,
        in_specs=[VMEM],
        out_specs=[HBM] * 4,
        out_shape=[cache, cache, scales, scales],
        scratch_shapes=[pltpu.VMEM((2, CAP, PAGE, sources), jnp.bfloat16), pltpu.SemaphoreType.DMA((4,))],
        compiler_params=pltpu.CompilerParams(vmem_limit_bytes=8 * 2**20),
        cost_estimate=CHEAP,
        name="unpack",
    )(received)
    return (
        cache_keys,
        cache_values,
        key_scales.transpose(2, 0, 1)[:, None],
        value_scales.transpose(2, 0, 1)[:, None],
    )


def mask_kernel(lengths, bias):
    ctx = lax.axis_index("ctx")
    core = lax.rem(ctx, 2)
    query_pos = ctx * TOK + iota((TOK, TOK), 1)
    start = jnp.zeros((TOK, TOK), jnp.int32)
    end = jnp.int32(0)
    for r in range(REQS):
        end = end + lengths[0, r]
        start = jnp.where(query_pos >= end, end, start)
    back = (4, jnp.where(core == 0, 3, 1), 2, jnp.where(core == 0, 1, 3), 0)
    for b in range(BLOCKS):
        key_pos = (ctx - back[b]) * TOK + iota((TOK, TOK), 0)
        kept = (key_pos >= start) & (key_pos <= query_pos)
        bias[b * TOK : (b + 1) * TOK, :] = jnp.where(kept, 0.0, -1e30)


def mask(lengths):
    return pl.pallas_call(
        mask_kernel,
        in_specs=[SMEM],
        out_specs=VMEM,
        out_shape=jax.ShapeDtypeStruct((WINDOW, TOK), jnp.float32),
        cost_estimate=pl.CostEstimate(flops=2000000000, bytes_accessed=1000, transcendentals=0),
        compiler_params=pltpu.CompilerParams(vmem_limit_bytes=8 * 2**20),
        name="mask",
    )(lengths)


def attend_kernel(first, heads, bias, queries, *rest):
    out, q_buf, o_buf, sums, q_sem, o_sem = rest[-6:]
    def query_copy(h):
        at = pl.ds(pl.multiple_of(h * HEAD_WIDTH, HEAD_WIDTH), HEAD_WIDTH)
        from_at = pl.ds(pl.multiple_of((first + h) * HEAD_WIDTH, HEAD_WIDTH), HEAD_WIDTH)
        return pltpu.make_async_copy(queries.at[0, :, from_at], q_buf.at[:, at], q_sem.at[h])

    def out_copy(h, g0):
        width = STACK * HD
        at = pl.ds(pl.multiple_of(h * HEAD_WIDTH + g0 * HD, width), width)
        to_at = pl.ds(pl.multiple_of((first + h) * HEAD_WIDTH + g0 * HD, width), width)
        return pltpu.make_async_copy(o_buf.at[:, at], out.at[0, :, to_at], o_sem.at[h])

    for h in range(heads):
        query_copy(h).start()

    even = jnp.full((TOK, HD), lax.rem(lax.axis_index("ctx"), 2), jnp.int32) == 0
    sums[0] = jnp.ones((8, STACK * TOK), jnp.float32)
    sums[1] = jnp.ones((8, STACK * TOK), jnp.float32)
    ones = jnp.ones((16, WINDOW), jnp.bfloat16)
    def window(arrays, lanes):
        own, beside, near, near_beside, far, far_beside = (array[0, :, lanes] for array in arrays)
        third = jnp.where(even, far_beside, beside)
        return jnp.concatenate([far, third, near, near_beside, own], 0)

    def one_head(h, stack, with_top):
        lanes = pl.ds(pl.multiple_of((first + h) * HD, HD), HD)
        key_rows, value_rows = window(rest[0:12:2], lanes), window(rest[1:12:2], lanes)
        value_side = jnp.concatenate([value_rows.T, ones], 0)
        mask = jnp.concatenate([bias[...]] * stack, 1)

        def head_lanes(h, g):
            return pl.ds(pl.multiple_of(h * HEAD_WIDTH + g * HD, HD), HD)

        def score(g0):
            rows = jnp.concatenate([q_buf[:, head_lanes(h, g0 + g)] for g in range(stack)], 0)
            return lax.dot_general(key_rows, rows, NT, preferred_element_type=jnp.float32)

        def finish(g0, scores):
            if with_top:
                masked = scores + mask
                exponent = (masked - jnp.max(masked, axis=0, keepdims=True)) * EXP_SCALE
            else:
                exponent = scores * EXP_SCALE + mask
            weights = jnp.exp2(exponent).astype(jnp.bfloat16)
            mixed = lax.dot_general(value_side, weights, NN, preferred_element_type=jnp.float32)
            if not with_top:
                total = mixed[HD : HD + 8]
                sums[0] = jnp.minimum(sums[0], total)
                sums[1] = jnp.maximum(sums[1], total)
            result = (mixed[:HD] * (1.0 / mixed[HD : HD + 1])).astype(jnp.bfloat16)
            for g in range(stack):
                o_buf[:, head_lanes(h, g0 + g)] = result[:, g * TOK : (g + 1) * TOK].T
            if (g0 + stack) % STACK == 0:
                out_copy(h, g0 + stack - STACK).start()

        scores = score(0)
        for g0 in range(0, GROUP, stack):
            following = score(g0 + stack) if g0 + stack < GROUP else None
            finish(g0, scores)
            scores = following

    def first_pass(h, carry):
        query_copy(h).wait()
        one_head(h, STACK, False)
        return carry

    def wait_out(h, carry):
        for g0 in range(0, GROUP, STACK):
            out_copy(h, g0).wait()
        return carry

    lax.fori_loop(0, heads, first_pass, 0)
    lax.fori_loop(0, heads, wait_out, 0)

    in_range = (jnp.min(sums[0]) > SUM_LEAST) & (jnp.max(sums[1]) < SUM_MOST)

    @pl.when(jnp.logical_not(in_range))
    def _():
        def second_pass(h, carry):
            one_head(h, STACK_TOP, True)
            return wait_out(h, carry)

        lax.fori_loop(0, heads, second_pass, 0)


def attend(first, heads, bias, queries, *operands, partial=None):
    more = () if partial is None else (partial,)
    return pl.pallas_call(
        functools.partial(attend_kernel, first, heads),
        in_specs=[VMEM, HBM] + [VMEM] * len(operands) + [HBM] * len(more),
        out_specs=HBM,
        out_shape=jax.ShapeDtypeStruct(queries.shape, jnp.bfloat16),
        scratch_shapes=[
            pltpu.VMEM((TOK, heads * HEAD_WIDTH), jnp.bfloat16),
            pltpu.VMEM((TOK, heads * HEAD_WIDTH), jnp.bfloat16),
            pltpu.VMEM((2, 8, STACK * TOK), jnp.float32),
            pltpu.SemaphoreType.DMA((heads,)),
            pltpu.SemaphoreType.DMA((heads,)),
        ],
        input_output_aliases={2 + len(operands): 0} if more else {},
        compiler_params=pltpu.CompilerParams(vmem_limit_bytes=50 * 2**20),
        cost_estimate=pl.CostEstimate(flops=6000000000, bytes_accessed=1000, transcendentals=0),
        name=f"attend{first}",
    )(bias, queries, *operands, *more)


def body(queries, keys, values, lengths, owners):
    ctx_count = lax.axis_size("ctx")

    def chips_on(block, chips):
        step = 2 * chips
        return lax.ppermute(block, "ctx", [(i, (i + step) % ctx_count) for i in range(ctx_count)])

    def swap(block):
        return lax.ppermute(block, "ctx", [(i, i ^ 1) for i in range(ctx_count)])

    near_values = chips_on(values, 1)
    ahead_keys = chips_on(keys, -1)
    near_keys = chips_on(keys, 1)

    message = pack(owners.reshape(PAGES_DEV), keys, values)
    lengths, message = lax.optimization_barrier((lengths, message))
    bias = mask(lengths)
    near_values, ahead_keys, message, bias = lax.optimization_barrier((near_values, ahead_keys, message, bias))
    far_values = chips_on(near_values, 1)
    far_keys = chips_on(ahead_keys, -1)
    received = lax.all_to_all(message, ("ctx", "dec"), split_axis=0, concat_axis=0, tiled=True)

    near_keys, near_values, far_keys, far_values, own = lax.optimization_barrier(
        (near_keys, near_values, far_keys, far_values, (keys, values))
    )
    beside = (swap(own[0]), swap(own[1]))
    near = (near_keys, near_values)
    far = (far_keys, far_values)
    near_beside = (swap(near_keys), swap(near_values))
    far_beside = (swap(far_keys), swap(far_values))
    attended = None
    for first, heads in PARTS:
        attended = attend(
            first, heads, bias, queries, keys, values, *beside, *near, *near_beside, *far, *far_beside, partial=attended
        )
    attended, received = lax.optimization_barrier((attended, received))
    return (attended,) + unpack(received)


def solution(mesh):
    placed = (
        P("dec", "ctx", None),
        P("dec", "ctx", None),
        P("dec", "ctx", None),
        P("dec", None),
        P("dec", "ctx", None),
    )
    return jax.shard_map(
        body,
        mesh=mesh,
        in_specs=placed,
        out_specs=(
            P("dec", "ctx", None),
            P(None, "ctx", "dec", None),
            P(None, "ctx", "dec", None),
            P(None, "ctx", "dec", None),
            P(None, "ctx", "dec", None),
        ),
        check_vma=False,
    )
```

```python
import functools
import math

import jax
import jax.numpy as jnp
from jax import lax
from jax.experimental import pallas as pl
from jax.experimental.pallas import tpu as pltpu
from jax.sharding import PartitionSpec as P

HD = 128
KVH = 8
GROUP = 16
PAGE = 8
CAP = 2
REQS = 4
TOK = 128
PAGES_DEV = 16
OWNERS = 16
BLOCKS = 5
WINDOW = BLOCKS * TOK
ROW = 2 * PAGE * HD + HD
STACK = 8
STACK_TOP = 4
HEAD_WIDTH = GROUP * HD
SUM_LEAST = 2.0**-100
SUM_MOST = 2.0**100
PARTS = ((0, 8),)
EXP_SCALE = math.log2(math.e) / math.sqrt(HD)
INV_ROOT = 1.0 / math.sqrt(HD)
NT = (((1,), (1,)), ((), ()))
NN = (((1,), (0,)), ((), ()))
CHEAP = pl.CostEstimate(flops=1000, bytes_accessed=1000, transcendentals=0)
HBM = pl.BlockSpec(memory_space=pltpu.HBM)
SMEM = pl.BlockSpec(memory_space=pltpu.SMEM)
VMEM = pl.BlockSpec(memory_space=pltpu.VMEM)


def iota(shape, axis):
    return lax.broadcasted_iota(jnp.int32, shape, axis)


def pack_kernel(owners, keys, values, out, held, sem):
    row, col = iota((HD, HD), 0), iota((HD, HD), 1)
    common = row & col
    parity = jnp.zeros((HD, HD), jnp.int32)
    for bit in range(7):
        parity = parity + ((common >> bit) & 1)
    signs = (1 - 2 * (parity & 1)).astype(jnp.float32).astype(jnp.bfloat16)
    position = iota((1, TOK), 1)
    page, within = position // PAGE, position % PAGE
    slot = jnp.zeros((1, TOK), jnp.int32)
    for p in range(PAGES_DEV):
        rank = jnp.int32(0)
        for q in range(p):
            rank = rank + (owners[q] == owners[p]).astype(jnp.int32)
        slot = jnp.where(page == p, owners[p] * CAP + rank, slot)
    slots = OWNERS * CAP
    place = iota((PAGE * slots, TOK), 0)
    select = jnp.where((place % slots == slot) & (place // slots == within), 1.0, 0.0).astype(jnp.bfloat16)
    any_row = jnp.where(iota((slots, TOK), 0) == slot, 1.0, 0.0).astype(jnp.bfloat16)
    lane, in_page = iota((TOK, HD), 1), iota((TOK, HD), 0) % PAGE
    def put(h, at, tile):
        held[h * OWNERS : (h + 1) * OWNERS, :, at : at + HD] = tile.reshape(OWNERS, CAP, HD).astype(jnp.bfloat16)

    def head_copy(h):
        rows = pl.ds(h * OWNERS, OWNERS)
        return pltpu.make_async_copy(held.at[rows], out.at[rows], sem.at[h])

    for h in range(KVH):
        scales = jnp.zeros((TOK, HD), jnp.float32)
        codes = []
        for which, rows in enumerate((keys, values)):
            rotated = (
                lax.dot_general(rows[0, :, h * HD : (h + 1) * HD], signs, NN, preferred_element_type=jnp.float32)
                * INV_ROOT
            )
            scale = (jnp.max(jnp.abs(rotated), axis=-1, keepdims=True) + 1e-06).astype(jnp.bfloat16)
            scale = scale.astype(jnp.float32)
            codes.append((rotated * (1.0 / scale)).astype(jnp.bfloat16))
            scales = jnp.where(lane == which * PAGE + in_page, scale, scales)
        placed = lax.dot_general(select, jnp.concatenate(codes, 1), NN, preferred_element_type=jnp.float32)
        for which in range(2):
            for i in range(PAGE):
                put(h, (which * PAGE + i) * HD, placed[i * slots : (i + 1) * slots, which * HD : (which + 1) * HD])
        scales = lax.dot_general(any_row, scales.astype(jnp.bfloat16), NN, preferred_element_type=jnp.float32)
        put(h, 2 * PAGE * HD, scales)
        head_copy(h).start()
    for h in range(KVH):
        head_copy(h).wait()


def pack(owners, keys, values):
    shape = (KVH * OWNERS, CAP, ROW)
    return pl.pallas_call(
        pack_kernel,
        in_specs=[SMEM, VMEM, VMEM],
        out_specs=HBM,
        out_shape=jax.ShapeDtypeStruct(shape, jnp.bfloat16),
        scratch_shapes=[pltpu.VMEM(shape, jnp.bfloat16), pltpu.SemaphoreType.DMA((KVH,))],
        compiler_params=pltpu.CompilerParams(vmem_limit_bytes=60 * 2**20),
        cost_estimate=CHEAP,
        name="pack",
    )(owners, keys, values)


def unpack_kernel(received, cache_keys, cache_values, key_scales, value_scales, held, sem):
    half = PAGE * HD
    copies = [
        pltpu.make_async_copy(received.at[:, :, pl.ds(0, half)], cache_keys.at[:, 0], sem.at[0]),
        pltpu.make_async_copy(received.at[:, :, pl.ds(half, half)], cache_values.at[:, 0], sem.at[1]),
        pltpu.make_async_copy(held.at[0], key_scales, sem.at[2]),
        pltpu.make_async_copy(held.at[1], value_scales, sem.at[3]),
    ]
    copies[0].start()
    copies[1].start()
    for slot in range(CAP):
        turned = received[:, slot, 2 * half :].T
        held[0, slot] = turned[:PAGE]
        held[1, slot] = turned[PAGE : 2 * PAGE]
    copies[2].start()
    copies[3].start()
    for copy in copies:
        copy.wait()


def unpack(received):
    sources = received.shape[0]
    cache = jax.ShapeDtypeStruct((sources, 1, CAP, PAGE * HD), jnp.bfloat16)
    scales = jax.ShapeDtypeStruct((CAP, PAGE, sources), jnp.bfloat16)
    cache_keys, cache_values, key_scales, value_scales = pl.pallas_call(
        unpack_kernel,
        in_specs=[VMEM],
        out_specs=[HBM] * 4,
        out_shape=[cache, cache, scales, scales],
        scratch_shapes=[pltpu.VMEM((2, CAP, PAGE, sources), jnp.bfloat16), pltpu.SemaphoreType.DMA((4,))],
        compiler_params=pltpu.CompilerParams(vmem_limit_bytes=8 * 2**20),
        cost_estimate=CHEAP,
        name="unpack",
    )(received)
    return (
        cache_keys,
        cache_values,
        key_scales.transpose(2, 0, 1)[:, None],
        value_scales.transpose(2, 0, 1)[:, None],
    )


def mask_kernel(lengths, bias):
    ctx = lax.axis_index("ctx")
    core = lax.rem(ctx, 2)
    query_pos = ctx * TOK + iota((TOK, TOK), 1)
    start = jnp.zeros((TOK, TOK), jnp.int32)
    end = jnp.int32(0)
    for r in range(REQS):
        end = end + lengths[0, r]
        start = jnp.where(query_pos >= end, end, start)
    back = (4, jnp.where(core == 0, 3, 1), 2, jnp.where(core == 0, 1, 3), 0)
    for b in range(BLOCKS):
        key_pos = (ctx - back[b]) * TOK + iota((TOK, TOK), 0)
        kept = (key_pos >= start) & (key_pos <= query_pos)
        bias[b * TOK : (b + 1) * TOK, :] = jnp.where(kept, 0.0, -1e30)


def mask(lengths):
    return pl.pallas_call(
        mask_kernel,
        in_specs=[SMEM],
        out_specs=VMEM,
        out_shape=jax.ShapeDtypeStruct((WINDOW, TOK), jnp.float32),
        cost_estimate=pl.CostEstimate(flops=2000000000, bytes_accessed=1000, transcendentals=0),
        compiler_params=pltpu.CompilerParams(vmem_limit_bytes=8 * 2**20),
        name="mask",
    )(lengths)


def attend_kernel(first, heads, bias, queries, *rest):
    out, o_buf, sums, o_sem = rest[-4:]
    def out_copy(h, g0):
        width = STACK * HD
        at = pl.ds(pl.multiple_of(h * HEAD_WIDTH + g0 * HD, width), width)
        to_at = pl.ds(pl.multiple_of((first + h) * HEAD_WIDTH + g0 * HD, width), width)
        return pltpu.make_async_copy(o_buf.at[:, at], out.at[0, :, to_at], o_sem.at[h])

    even = jnp.full((TOK, HD), lax.rem(lax.axis_index("ctx"), 2), jnp.int32) == 0
    sums[0] = jnp.ones((8, STACK * TOK), jnp.float32)
    sums[1] = jnp.ones((8, STACK * TOK), jnp.float32)
    ones = jnp.ones((16, WINDOW), jnp.bfloat16)
    def window(arrays, lanes):
        own, beside, near, near_beside, far, far_beside = (array[0, :, lanes] for array in arrays)
        third = jnp.where(even, far_beside, beside)
        return jnp.concatenate([far, third, near, near_beside, own], 0)

    def one_head(h, stack, with_top):
        lanes = pl.ds(pl.multiple_of((first + h) * HD, HD), HD)
        key_rows, value_rows = window(rest[0:12:2], lanes), window(rest[1:12:2], lanes)
        value_side = jnp.concatenate([value_rows.T, ones], 0)
        mask = jnp.concatenate([bias[...]] * stack, 1)

        def head_lanes(h, g):
            return pl.ds(pl.multiple_of(h * HEAD_WIDTH + g * HD, HD), HD)

        def score(g0):
            rows = jnp.concatenate([queries[0, :, head_lanes(first + h, g0 + g)] for g in range(stack)], 0)
            return lax.dot_general(key_rows, rows, NT, preferred_element_type=jnp.float32)

        def finish(g0, scores):
            if with_top:
                masked = scores + mask
                exponent = (masked - jnp.max(masked, axis=0, keepdims=True)) * EXP_SCALE
            else:
                exponent = scores * EXP_SCALE + mask
            weights = jnp.exp2(exponent).astype(jnp.bfloat16)
            mixed = lax.dot_general(value_side, weights, NN, preferred_element_type=jnp.float32)
            if not with_top:
                total = mixed[HD : HD + 8]
                sums[0] = jnp.minimum(sums[0], total)
                sums[1] = jnp.maximum(sums[1], total)
            result = (mixed[:HD] * (1.0 / mixed[HD : HD + 1])).astype(jnp.bfloat16)
            for g in range(stack):
                o_buf[:, head_lanes(h, g0 + g)] = result[:, g * TOK : (g + 1) * TOK].T
            if (g0 + stack) % STACK == 0:
                out_copy(h, g0 + stack - STACK).start()

        scores = score(0)
        for g0 in range(0, GROUP, stack):
            following = score(g0 + stack) if g0 + stack < GROUP else None
            finish(g0, scores)
            scores = following

    def first_pass(h, carry):
        one_head(h, STACK, False)
        return carry

    def wait_out(h, carry):
        for g0 in range(0, GROUP, STACK):
            out_copy(h, g0).wait()
        return carry

    lax.fori_loop(0, heads, first_pass, 0)
    lax.fori_loop(0, heads, wait_out, 0)

    in_range = (jnp.min(sums[0]) > SUM_LEAST) & (jnp.max(sums[1]) < SUM_MOST)

    @pl.when(jnp.logical_not(in_range))
    def _():
        def second_pass(h, carry):
            one_head(h, STACK_TOP, True)
            return wait_out(h, carry)

        lax.fori_loop(0, heads, second_pass, 0)


def attend(first, heads, bias, queries, *operands, partial=None):
    more = () if partial is None else (partial,)
    return pl.pallas_call(
        functools.partial(attend_kernel, first, heads),
        in_specs=[VMEM, VMEM] + [VMEM] * len(operands) + [HBM] * len(more),
        out_specs=HBM,
        out_shape=jax.ShapeDtypeStruct(queries.shape, jnp.bfloat16),
        scratch_shapes=[
            pltpu.VMEM((TOK, heads * HEAD_WIDTH), jnp.bfloat16),
            pltpu.VMEM((2, 8, STACK * TOK), jnp.float32),
            pltpu.SemaphoreType.DMA((heads,)),
        ],
        input_output_aliases={2 + len(operands): 0} if more else {},
        compiler_params=pltpu.CompilerParams(vmem_limit_bytes=28 * 2**20),
        cost_estimate=pl.CostEstimate(flops=6000000000, bytes_accessed=1000, transcendentals=0),
        name=f"attend{first}",
    )(bias, queries, *operands, *more)


def body(queries, keys, values, lengths, owners):
    ctx_count = lax.axis_size("ctx")

    def chips_on(block, chips):
        step = 2 * chips
        return lax.ppermute(block, "ctx", [(i, (i + step) % ctx_count) for i in range(ctx_count)])

    def swap(block):
        return lax.ppermute(block, "ctx", [(i, i ^ 1) for i in range(ctx_count)])

    near_values = chips_on(values, 1)
    ahead_keys = chips_on(keys, -1)
    near_keys = chips_on(keys, 1)

    message = pack(owners.reshape(PAGES_DEV), keys, values)
    near_values, message = lax.optimization_barrier((near_values, message))
    far_values = chips_on(near_values, 1)
    ahead_keys, lengths, message = lax.optimization_barrier((ahead_keys, lengths, message))
    far_keys = chips_on(ahead_keys, -1)
    bias = mask(lengths)
    received = lax.all_to_all(message, ("ctx", "dec"), split_axis=0, concat_axis=0, tiled=True)

    near_keys, near_values, far_keys, far_values, own = lax.optimization_barrier(
        (near_keys, near_values, far_keys, far_values, (keys, values))
    )
    beside = (swap(own[0]), swap(own[1]))
    near = (near_keys, near_values)
    far = (far_keys, far_values)
    near_beside = (swap(near_keys), swap(near_values))
    far_beside = (swap(far_keys), swap(far_values))
    attended = None
    for first, heads in PARTS:
        attended = attend(
            first, heads, bias, queries, keys, values, *beside, *near, *near_beside, *far, *far_beside, partial=attended
        )
    attended, received = lax.optimization_barrier((attended, received))
    return (attended,) + unpack(received)


def solution(mesh):
    placed = (
        P("dec", "ctx", None),
        P("dec", "ctx", None),
        P("dec", "ctx", None),
        P("dec", None),
        P("dec", "ctx", None),
    )
    return jax.shard_map(
        body,
        mesh=mesh,
        in_specs=placed,
        out_specs=(
            P("dec", "ctx", None),
            P(None, "ctx", "dec", None),
            P(None, "ctx", "dec", None),
            P(None, "ctx", "dec", None),
            P(None, "ctx", "dec", None),
        ),
        check_vma=False,
    )
```
